32 devices in a mesh: dp: 16 (over z, x, core), mp: 2 (over y).
Axes of the slice: x: 2, y: 2, z: 4, core: 2. Of those that a mesh axis runs over, the one named last changes fastest.
Arguments:
- inputs: bfloat16 [16, 1024, 512], P('dp'), may hold values from -6 to 6
- segment_ids: int32 [16, 1024], P('dp'), may hold values from 0 to 3, never falling along the last dimension, each value on 1 to 512 neighbouring positions
- attention_norm_scale: float32 [512], replicated, may hold values from 0.25 to 1.75
- attention_norm_bias: float32 [512], replicated, may hold values from -3 to 3
- qkv_weight: bfloat16 [512, 8, 192], P(None, 'mp'), may hold values from -0.25 to 0.25
- qkv_bias: float32 [8, 192], P('mp'), may hold values from -3 to 3
- out_weight: bfloat16 [8, 64, 512], P('mp'), may hold values from -1 to 1
- out_bias: float32 [512], replicated, may hold values from -3 to 3
- feedforward_norm_scale: float32 [512], replicated, may hold values from 0.25 to 1.75
- feedforward_norm_bias: float32 [512], replicated, may hold values from -3 to 3
- in_weight: bfloat16 [512, 2048], P(None, 'mp'), may hold values from -0.25 to 0.25
- in_bias: float32 [2048], P('mp'), may hold values from -3 to 3
- down_weight: bfloat16 [2048, 512], P('mp'), may hold values from -0.125 to 0.125
- down_bias: float32 [512], replicated, may hold values from -3 to 3
- cotangent: bfloat16 [16, 1024, 512], P('dp'), may hold values from -6 to 6
Outputs:
- outputs: float32 [16, 1024, 512], P('dp', 'mp')
- input_grad: float32 [16, 1024, 512], P('dp', 'mp')
- attn_norm_gain_grad: float32 [512], replicated
- attn_norm_shift_grad: float32 [512], replicated
- qkv_weight_grad: float32 [512, 8, 192], P(None, 'mp')
- qkv_bias_grad: float32 [8, 192], P('mp')
- out_weight_grad: float32 [8, 64, 512], P('mp')
- out_bias_grad: float32 [512], replicated
- ffn_norm_gain_grad: float32 [512], replicated
- ffn_norm_shift_grad: float32 [512], replicated
- in_weight_grad: float32 [512, 2048], P(None, 'mp')
- in_bias_grad: float32 [2048], P('mp')
- down_weight_grad: float32 [2048, 512], P('mp')
- down_bias_grad: float32 [512], replicated
The draws below stay inside these ranges and needn't reach their ends.
Inputs may be any that keep to these rules, and one draw needn't show every extreme that they name: `segment_ids`: in each row the ids never fall and every gene has 1 to 512 codons; in every draw some gene has exactly 512.
All inputs are finite; a program needn't handle non-finite values.
Results may differ from the reference program's by a relative error of at most 0.019.
Values may be sent and summed in bfloat16 or wider, within the bound.
A program may use at most 128 MiB of HBM per device.

```python
import math
import jax
import jax.numpy as jnp
import numpy as np
from jax import lax

D = 512
HEADS = 8
HD = 64
FF = 2048
L = 1024
GENES = 4
ROWS = 16


def block_scale(own_key, shape, cuts, smallest, top_value):
    def one(position, blocks):
        heights = jax.random.uniform(jax.random.fold_in(jax.random.fold_in(own_key, 6), position), (blocks,), jnp.float32, smallest / len(cuts), top_value / len(cuts))
        return jnp.repeat(jnp.exp(heights), shape[position] // blocks).reshape((-1,) + (1,) * (len(shape) - position - 1))

    level = one(*cuts[0])
    for cut in cuts[1:]:
        level = level * one(*cut)
    return level


def split_up(amount, total, bound, slope):
    weights = [(1 << 20) // math.isqrt(standing ** slope) + 1 for standing in range(2, amount + 1)]
    spare, given = total - bound - (amount - 1), [1] * (amount - 1)
    while spare > 0:
        candidates = [i for i in range(amount - 1) if given[i] < bound]
        mass, budget = sum([weights[i] for i in candidates]), spare
        for i in candidates:
            extra = min(bound - given[i], max(1, budget * weights[i] // mass), spare)
            given[i] = given[i] + extra
            spare = spare - extra
    return np.array([bound] + given)


def ragged_sizes(own_key, amount, total, most, slope):
    if amount == 2:
        one = jax.random.randint(own_key, (), max(1, total - most), min(most, total - 1) + 1)
        return jnp.stack([one, total - one])
    sizes = jnp.asarray(split_up(amount, total, most, slope), jnp.int32)
    twos = (amount - 1) // 2
    donor, receiver = sizes[1:1 + 2 * twos:2], sizes[2:2 + 2 * twos:2]
    slack = jnp.minimum(donor - 1, most - receiver)
    moved = jax.random.randint(jax.random.fold_in(own_key, 1), (twos,), 0, 1 << 20) % (slack + 1)
    sizes = sizes.at[1:1 + 2 * twos:2].set(donor - moved).at[2:2 + 2 * twos:2].set(receiver + moved)
    return sizes[jax.random.permutation(jax.random.fold_in(own_key, 2), amount)]


def scatter_about(stream_key, dims, width, limit, cuts=(), held_as=jnp.bfloat16):
    array = width * jax.random.normal(stream_key, dims, jnp.float32)
    if cuts:
        array = array * block_scale(stream_key, dims, cuts, -0.22, 0.18)
    return jnp.clip(array, -limit, limit).astype(held_as)


def setup_inputs(seed: int = 0) -> dict:
    seeds = jax.random.split(jax.random.key(seed), 16)
    return {
        "inputs": scatter_about(seeds[0], (ROWS, L, D), 1.0, 6.0, ((0, 16),)),
        "segment_ids": jax.vmap(lambda own: jnp.searchsorted(jnp.cumsum(ragged_sizes(own, GENES, L, L // 2, 0)), jnp.arange(L), side="right"))(jax.random.split(seeds[1], ROWS)).reshape((ROWS, L)).astype(jnp.int32),
        "attention_norm_scale": jnp.clip(1.0 + 0.15 * jax.random.normal(seeds[2], (D,), jnp.float32), 0.25, 1.75),
        "attention_norm_bias": scatter_about(seeds[3], (D,), 0.3, 3.0, (), jnp.float32),
        "qkv_weight": scatter_about(seeds[4], (D, HEADS, 3 * HD), D ** -0.5, 0.25, ((1, 2),)),
        "qkv_bias": scatter_about(seeds[5], (HEADS, 3 * HD), 0.5, 3.0, ((0, 2),), jnp.float32),
        "out_weight": scatter_about(seeds[6], (HEADS, HD, D), (HEADS * HD // 16) ** -0.5, 1.0, ((0, 2),)),
        "out_bias": scatter_about(seeds[7], (D,), 0.3, 3.0, (), jnp.float32),
        "feedforward_norm_scale": jnp.clip(1.0 + 0.15 * jax.random.normal(seeds[8], (D,), jnp.float32), 0.25, 1.75),
        "feedforward_norm_bias": scatter_about(seeds[9], (D,), 0.3, 3.0, (), jnp.float32),
        "in_weight": scatter_about(seeds[10], (D, FF), D ** -0.5, 0.25, ((1, 2),)),
        "in_bias": scatter_about(seeds[11], (FF,), 0.5, 3.0, ((0, 2),), jnp.float32),
        "down_weight": scatter_about(seeds[12], (FF, D), FF ** -0.5, 0.125, ((0, 2),)),
        "down_bias": scatter_about(seeds[13], (D,), 0.3, 3.0, (), jnp.float32),
        "cotangent": scatter_about(seeds[14], (ROWS, L, D), 1.0, 6.0, ((0, 16),)),
    }


EPS = 1e-05
NEG = -1e+30
HIGHEST = lax.Precision.HIGHEST

@jax.custom_vjp
def low(v):
    return lax.optimization_barrier(v.astype(jnp.bfloat16)).astype(jnp.float32)

@jax.custom_vjp
def low_back(v):
    return v

def low_keep(v):
    return (low(v), None)

def low_pass(kept, grad):
    return (grad,)

def back_keep(v):
    return (v, None)

def back_low(kept, grad):
    return (low(grad),)
low.defvjp(low_keep, low_pass)
low_back.defvjp(back_keep, back_low)

def normalize_rows(values):
    centered = values - lax.optimization_barrier(jnp.mean(values, -1, keepdims=True))
    return centered * lax.rsqrt(lax.optimization_barrier(jnp.mean(centered * centered, -1, keepdims=True)) + EPS)

def rotate(vectors, count):
    half_size = vectors.shape[-1] // 2
    freq_index = jnp.arange(half_size, dtype=jnp.float32)
    frequency = jnp.exp(freq_index * (-math.log(10000.0) / half_size))
    angles = jnp.arange(count, dtype=jnp.float32)[:, None] * frequency[None, :]
    cosine = jnp.cos(angles)[:, None, :]
    sines = jnp.sin(angles)[:, None, :]
    lower_half = vectors[..., :half_size]
    upper_half = vectors[..., half_size:]
    return jnp.concatenate([lower_half * cosine - upper_half * sines, upper_half * cosine + lower_half * sines], -1)

def arrange(projected):
    head_size = projected.shape[-1] // 3
    count = projected.shape[1]
    queries = rotate(projected[..., :head_size], count) * head_size ** (-0.5)
    rotated_keys = rotate(projected[..., head_size:2 * head_size], count)
    return (queries, rotated_keys, projected[..., 2 * head_size:])

def attend_row(row_args):
    queries, rotated_keys, values, segments = row_args
    scores = low_back(jnp.einsum('qhe,khe->hqk', queries, rotated_keys, precision=HIGHEST))
    same_gene = (segments[:, None] == segments[None, :])[None]
    scores = jnp.where(same_gene, scores, NEG)
    row_max = lax.optimization_barrier(jnp.max(scores, -1, keepdims=True))
    exp_scores = jnp.exp(scores - row_max)
    probability = exp_scores / lax.optimization_barrier(jnp.sum(exp_scores, -1, keepdims=True))
    return jnp.einsum('hqk,khe->qhe', low(probability), values, precision=HIGHEST)

def forward(layer_input_rows, gain_one, shift_one, qkv_w, qkv_b, out_w, out_b, gain_two, shift_two, in_w, in_b, down_w, down_b, segment_ids):
    normed = low(normalize_rows(layer_input_rows) * gain_one + shift_one)
    projected = low_back(jnp.einsum('rld,dhe->rlhe', normed, qkv_w, precision=HIGHEST) + qkv_b)
    queries, rotated_keys, values = arrange(projected)
    queries = low(queries)
    rotated_keys = low(rotated_keys)
    values = low(values)
    attended = lax.map(jax.checkpoint(attend_row), (queries, rotated_keys, values, segment_ids))
    attended = low(low_back(attended))
    branch = low_back(jnp.einsum('rlhe,hed->rld', attended, out_w, precision=HIGHEST) + out_b)
    hidden_after_attention = layer_input_rows + branch
    second_normed_rows = low(normalize_rows(hidden_after_attention) * gain_two + shift_two)
    hidden = low_back(jnp.einsum('rld,df->rlf', second_normed_rows, in_w, precision=HIGHEST) + in_b)
    active = low(jax.nn.gelu(hidden, approximate=False))
    result = low_back(jnp.einsum('rlf,fd->rld', active, down_w, precision=HIGHEST) + down_b)
    return hidden_after_attention + result

def reference(inputs, segment_ids, attention_norm_scale, attention_norm_bias, qkv_weight, qkv_bias, out_weight, out_bias, feedforward_norm_scale, feedforward_norm_bias, in_weight, in_bias, down_weight, down_bias, cotangent):

    def whole_layer(layer_input_rows, gain_one, shift_one, qkv_w, qkv_b, out_w, out_b, gain_two, shift_two, in_w, in_b, down_w, down_b):
        return forward(layer_input_rows, gain_one, shift_one, qkv_w, qkv_b, out_w, out_b, gain_two, shift_two, in_w, in_b, down_w, down_b, segment_ids)
    outputs, pull = jax.vjp(whole_layer, inputs.astype(jnp.float32), attention_norm_scale, attention_norm_bias, qkv_weight.astype(jnp.float32), qkv_bias, out_weight.astype(jnp.float32), out_bias, feedforward_norm_scale, feedforward_norm_bias, in_weight.astype(jnp.float32), in_bias, down_weight.astype(jnp.float32), down_bias)
    grads = pull(cotangent.astype(jnp.float32))
    return (outputs, grads[0], grads[1], grads[2], grads[3], grads[4], grads[5], grads[6], grads[7], grads[8], grads[9], grads[10], grads[11], grads[12])
```

```python
import functools
import math

import jax
import jax.numpy as jnp
import numpy as np
from jax import lax
from jax.experimental import pallas as pl
from jax.experimental.pallas import tpu as pltpu
from jax.sharding import PartitionSpec as P

f32, bf = jnp.float32, jnp.bfloat16
EPS = 1e-5
BIG = 1e30
LOG2E = math.log2(math.e)
AUG = 16
ERFCX_P = 0.425
ERFCX = (
    0.23971980880709728, 0.24117083247455387, 0.20509840538640725, 0.239985627333635,
    -0.07373126048981057, 0.3746498195367672, -0.29358684214803077, 0.06669325662319364,
)
MESH = pl.DeviceIdType.MESH
CHUNKS = ((0, 1024), (1024, 1024), (2048, 256), (2304, 768))
MODES = ("yx", "yx", "yx", "yx")
ROWS_SIDE = 3072


def dg(a, b, ca, cb):
    return lax.dot_general(a, b, (((ca,), (cb,)), ((), ())), preferred_element_type=f32)


def gelu_parts(u):
    ex = jnp.exp2(u * u * (-0.5 * LOG2E))
    t = 1.0 / (1.0 + (ERFCX_P / math.sqrt(2.0)) * jnp.abs(u))
    poly = 0.5 * ERFCX[-1]
    for c in ERFCX[-2::-1]:
        poly = poly * t + 0.5 * c
    tail = poly * t * ex
    phi_cum = jnp.where(u >= 0, 1.0 - tail, tail)
    return u * phi_cum, phi_cum + u * ex * (1.0 / math.sqrt(2 * math.pi))


def norm_rows(x):
    c = x - jnp.mean(x, -1, keepdims=True)
    rs = lax.rsqrt(jnp.mean(c * c, -1, keepdims=True) + EPS)
    return c * rs, rs


class Comm:
    def __init__(self, ssem, rsem):
        d, self.y = lax.axis_index("dp"), lax.axis_index("mp")
        self.z, self.x, self.c = d // 4, (d // 2) % 2, d % 2
        self.ssem, self.rsem, self.n, self.started = ssem, rsem, 0, []

    def dev(self, z=None, x=None, y=None, c=None):
        z, x, y, c = (b if a is None else a for a, b in ((z, self.z), (x, self.x), (y, self.y), (c, self.c)))
        return ((z * 2 + x) * 2 + c, y)

    def core(self):
        return self.dev(c=1 - self.c)

    def yy(self):
        return self.dev(y=1 - self.y)

    def xx(self):
        return self.dev(x=1 - self.x)

    def zz(self, k):
        return self.dev(z=lax.rem(self.z + k, 4))

    def partners(self):
        return [self.core(), self.yy(), self.xx()] + [self.zz(k) for k in (1, 2, 3)]

    def copy(self, src, dst, target):
        i = self.n
        self.n += 1

        def make():
            return pltpu.make_async_remote_copy(
                src_ref=src, dst_ref=dst, send_sem=self.ssem.at[i], recv_sem=self.rsem.at[i],
                device_id=target, device_id_type=MESH)
        self.started.append(make)
        return make

    def drain(self):
        for make in self.started:
            make().wait_send()


def rows(start, size):
    return pl.ds(pl.multiple_of(start, 16), size)


def mega(x_h, seg_ref, g1_ref, b1_ref, wt_h, qb_ref, ow_h, ob_ref, g2_ref, b2_ref, iw_h, ib_ref, dw_h, db_ref, ct_h, cos_h, sin_h,
         out_ref, ig_ref, fin_ref, vout_ref,
         x_v, ct_v, cos_v, sin_v, wt, ow, iw, dw, qb, ib,
         normed, normed_t, kq, kk, kv, e_ref, att, attb, rr, dob, ds, gp, normed2, normed2t, xh2, acc_o, acc_g, gm,
         grad, cr, yr, xr, zr, gn_own, gn_oth, gn_in, vec, vcr, vyr, vxr, vzr,
         lsem, ssem, rsem):
    A, D = x_v.shape
    T = ct_v.shape[0]
    H = 8
    HD = 64
    RB = 256
    QB = 256
    cm = Comm(ssem, rsem)
    own0 = pl.multiple_of(cm.y * T, T)
    oth0 = pl.multiple_of((1 - cm.y) * T, T)
    starts = (own0, oth0)

    barrier = pltpu.get_barrier_semaphore()
    for t in cm.partners():
        pl.semaphore_signal(barrier, inc=1, device_id=t, device_id_type=MESH)

    loads = [
        (x_h.at[pl.ds(own0, T)], x_v.at[pl.ds(0, T)]), (x_h.at[pl.ds(oth0, T)], x_v.at[pl.ds(T, T)]),
        (wt_h, wt.at[0]), (cos_h.at[:, pl.ds(own0, T)], cos_v.at[0]), (cos_h.at[:, pl.ds(oth0, T)], cos_v.at[1]),
        (sin_h.at[:, pl.ds(own0, T)], sin_v.at[0]), (sin_h.at[:, pl.ds(oth0, T)], sin_v.at[1]),
        (ow_h, ow.at[0]), (ct_h.at[pl.ds(own0, T)], ct_v), (iw_h, iw.at[0]), (dw_h, dw.at[0]),
    ]
    loads = [pltpu.make_async_copy(s, d, lsem.at[i]) for i, (s, d) in enumerate(loads)]
    for c in loads:
        c.start()
    qb[0:4, :] = qb_ref[...]
    ib[0:1, :] = ib_ref[...]

    quarter = cm.c * 2 + cm.x
    qother = cm.c * 2 + (1 - cm.x)
    parts = []

    def piece(src, dst, cols, r0, total, subs):
        q = total // 4
        n = q // subs
        item = {"y": [], "x": []}
        for s in range(subs):
            a = rows(r0 + quarter * q + s * n, n)
            item["y"].append(cm.copy(src.at[a, cols], dst.at[a, cols], cm.yy()))
            item["x"].append(cm.copy(dst.at[a, cols], dst.at[a, cols], cm.xx()))
        h = rows(r0 + cm.c * (total // 2), total // 2)
        item["c"] = [cm.copy(dst.at[h, cols], dst.at[h, cols], cm.core())]
        return item

    full = pl.ds(0, D)
    g_wt = piece(wt_h, wt.at[1], full, 0, 768, 2)
    g_ow = piece(ow_h, ow.at[1], full, 0, 256, 1)
    g_iw = [piece(iw_h, iw.at[1], pl.ds(j * 512, 512), 0, 512, 1) for j in range(2)]
    g_dw = [piece(dw_h, dw.at[1], full, j * 512, 512, 1) for j in range(2)]
    g_qb = cm.copy(qb_ref, qb.at[pl.ds(8, 4)], cm.yy())
    g_ib = cm.copy(ib_ref, ib.at[pl.ds(8, 1)], cm.yy())
    gathers = [g_wt, g_ow, g_iw[0], g_dw[0], g_iw[1], g_dw[1]]

    def start_gather():
        for it in gathers:
            for mk in it["y"]:
                mk().start()
            if it is g_wt:
                g_qb().start()
                g_ib().start()

    def fwd_x(it, s=None):
        for i, (my, mx) in enumerate(zip(it["y"], it["x"])):
            if s is None or s == i:
                my().wait_recv()
                mx().start()

    def fwd_c(it):
        for mx in it["x"]:
            mx().wait_recv()
        it["c"][0]().start()

    def ready(it):
        it["c"][0]().wait_recv()

    def chunk_stages(k):
        r0, R = CHUNKS[k]
        h, q, p = R // 2, R // 4, R // 16
        own, oth = grad.at[0], grad.at[1]
        lo = r0 + cm.c * h
        keep = rows(lo, h)
        give = rows(r0 + (1 - cm.c) * h, h)
        slot = rows(r0 // 2, h)
        qx, qo = lo + cm.x * q, lo + (1 - cm.x) * q
        px = qx + cm.z * p
        st = {}
        core_oth = cm.copy(oth.at[give], cr.at[1, slot], cm.core())
        core_own = cm.copy(own.at[give], cr.at[0, slot], cm.core())
        zs = [cm.copy(own.at[rows(qx + lax.rem(cm.z + j, 4) * p, p)], zr.at[j - 1, rows(r0 // 16, p)], cm.zz(j)) for j in (1, 2, 3)]
        agz = [cm.copy(fin_ref.at[rows(px, p)], fin_ref.at[rows(px, p)], cm.zz(j)) for j in (1, 2, 3)]
        agx = cm.copy(fin_ref.at[rows(qx, q)], fin_ref.at[rows(qx, q)], cm.xx())
        agc = cm.copy(fin_ref.at[keep], fin_ref.at[keep], cm.core())
        st["oth"] = lambda: core_oth().start()
        st["own"] = lambda: core_own().start()
        ycp = cm.copy(oth.at[keep], yr.at[slot], cm.yy())
        xslot = rows(r0 // 4, q)
        xcp = cm.copy(own.at[rows(qo, q)], xr.at[xslot], cm.xx())

        def s_y():
            core_oth().wait_recv()
            oth[keep] = (oth[keep].astype(f32) + cr[1, slot].astype(f32)).astype(bf)
            ycp().start()

        def s_x():
            core_own().wait_recv()
            ycp().wait_recv()
            own[keep] = (own[keep].astype(f32) + cr[0, slot].astype(f32) + yr[slot].astype(f32)).astype(bf)
            xcp().start()

        def s_z():
            xcp().wait_recv()
            qq = rows(qx, q)
            own[qq] = (own[qq].astype(f32) + xr[xslot].astype(f32)).astype(bf)
            for c in zs:
                c().start()

        def s_agz():
            acc = own[rows(px, p)].astype(f32)
            for j, c in enumerate(zs):
                c().wait_recv()
                acc = acc + zr[j, rows(r0 // 16, p)].astype(f32)
            fin_ref[rows(px, p)] = acc.astype(bf)
            for c in agz:
                c().start()

        def s_agx():
            for c in agz:
                c().wait_recv()
            agx().start()

        def s_agc():
            agx().wait_recv()
            agc().start()

        def s_end():
            agc().wait_recv()

        st.update(y=s_y, x=s_x, z=s_z, agz=s_agz, agx=s_agx, agc=s_agc, end=s_end)
        return st

    red = [chunk_stages(k) for k in range(4)]
    gn_cp = cm.copy(gn_oth, gn_in, cm.yy())
    v_core = cm.copy(vec, vcr, cm.core())
    v_y = cm.copy(vec.at[1], vyr, cm.yy())
    v_x = cm.copy(vec.at[0], vxr, cm.xx())
    v_z = [cm.copy(vzr.at[cm.z], vzr.at[cm.z], cm.zz(j)) for j in (1, 2, 3)]

    def norm1(i):
        loads[i].wait()
        for r in range(0, T, RB):
            xh, _ = norm_rows(x_v[pl.ds(i * T + r, RB), :].astype(f32))
            normed[pl.ds(i * T + r, RB), :] = (xh * g1_ref[...] + b1_ref[...]).astype(bf)
        normed_t[:, i * T:(i + 1) * T] = normed[i * T:(i + 1) * T, :].T

    norm1(0)
    pl.semaphore_wait(barrier, 6)
    start_gather()
    norm1(1)

    row = lax.broadcasted_iota(jnp.int32, (AUG, T), 0)
    so = seg_ref[:, pl.ds(own0, T)]
    sth = seg_ref[:, pl.ds(oth0, T)]
    q_aug = jnp.where(row == so, 1.0, 0.0).astype(bf)
    k_aug = [jnp.where((row == s) | (row >= 4), 0.0, -BIG).astype(bf) for s in (so, sth)]
    v_aug = jnp.where(row < 2, 1.0, 0.0).astype(bf)
    for i in range(2, 7):
        loads[i].wait()

    fwd_hooks = {
        2: [lambda: fwd_x(g_wt)],
        4: [lambda: fwd_c(g_wt), lambda: fwd_x(g_ow), lambda: g_qb().wait_recv(), lambda: ready(g_wt)],
        5: [lambda: fwd_x(g_iw[0]), lambda: fwd_c(g_ow)],
        6: [lambda: fwd_x(g_dw[0])],
        7: [lambda: fwd_c(g_iw[0]), lambda: fwd_x(g_iw[1])],
    }

    def run_hooks(hooks, h):
        for k, fs in hooks.items():
            @pl.when(h == k)
            def _():
                for f in fs:
                    f()

    def head_fwd(h, carry):
        run_hooks(fwd_hooks, h)
        side, hh = h // 4, lax.rem(h, 4)
        w = wt[side, pl.ds(pl.multiple_of(hh * 192, 64), 192), :]
        bcol = jnp.broadcast_to(qb[pl.ds(side * 8 + hh, 1), :], (128, 192)).T
        bcol = jnp.concatenate([bcol] * (T // 128), axis=1)
        for i in range(2):
            cos, sin = cos_v[i], sin_v[i]
            lo = 0 if i == 0 else 64
            p = dg(w[lo:], normed_t[:, i * T:(i + 1) * T], 1, 0) + bcol[lo:]
            if i == 0:
                a, b = p[0:32], p[32:64]
                sc = LOG2E / math.sqrt(HD)
                kq[h, 0:32, :] = ((a * cos - b * sin) * sc).astype(bf)
                kq[h, 32:64, :] = ((b * cos + a * sin) * sc).astype(bf)
                kq[h, 64:, :] = q_aug
                p = p[64:]
            sl = slice(i * T, (i + 1) * T)
            a, b = p[0:32], p[32:64]
            kk[h, 0:32, sl] = (a * cos - b * sin).astype(bf)
            kk[h, 32:64, sl] = (b * cos + a * sin).astype(bf)
            kk[h, 64:, sl] = k_aug[i]
            kv[h, 0:64, sl] = p[64:].astype(bf)
            kv[h, 64:, sl] = v_aug
        for q0 in range(0, T, QB):
            s = dg(kk[h], kq[h, :, q0:q0 + QB], 0, 0)
            mx = jnp.max(s, axis=0, keepdims=True)
            e = jnp.exp2(s - mx).astype(bf)
            e_ref[h, :, q0:q0 + QB] = e
            o = dg(kv[h], e, 1, 0)
            r = 1.0 / o[64:65]
            rr[pl.ds(h, 1), q0:q0 + QB] = r
            o = o[:64] * r
            hs = pl.ds(pl.multiple_of(h * 64, 64), 64)
            att[hs, q0:q0 + QB] = o
            attb[hs, q0:q0 + QB] = o.astype(bf)
        return carry

    lax.fori_loop(0, H, head_fwd, 0)

    for i in (7, 8):
        loads[i].wait()
    ready(g_ow)
    fwd_c(g_dw[0])
    fwd_x(g_dw[1])
    mid = x_v[0:T, :].astype(f32) + ob_ref[...]
    for s in range(2):
        mid = mid + dg(attb[s * 256:(s + 1) * 256, :], ow[s], 0, 0)
    acc_o[...] = mid
    rs2 = []
    for r in range(0, T, RB):
        xh, rs = norm_rows(acc_o[r:r + RB, :])
        rs2.append(rs)
        xh2[r:r + RB, :] = xh
        normed2[r:r + RB, :] = (xh * g2_ref[...] + b2_ref[...]).astype(bf)
    normed2t[...] = normed2[...].T
    acc_o[...] += db_ref[...]
    acc_g[...] = jnp.zeros_like(acc_g)
    for i in (9, 10):
        loads[i].wait()
    ready(g_iw[0])
    ready(g_dw[0])
    g_ib().wait_recv()

    ffn_hooks = {
        1: [red[0]["oth"], lambda: fwd_c(g_iw[1]), lambda: fwd_c(g_dw[1])],
        2: [red[0]["own"], red[0]["y"], lambda: ready(g_iw[1]), lambda: ready(g_dw[1])],
        3: [red[1]["oth"]],
    }

    def ffn(f, carry):
        run_hooks(ffn_hooks, f)
        side, j = 1 - lax.rem(f, 2), f // 2
        cols = pl.ds(pl.multiple_of(j * 512, 512), 512)
        w, d = iw[side, :, cols], dw[side, cols, :]
        u = dg(normed2[...], w, 1, 0) + ib[pl.ds(side * 8, 1), cols]
        act, dge = gelu_parts(u)
        act = act.astype(bf)
        acc_o[...] += dg(act, d, 1, 0)
        ga = dg(ct_v[...], d, 1, 1)
        gh = (ga * dge).astype(bf)
        acc_g[...] += dg(gh, w, 1, 1)
        r0 = pl.multiple_of(j * 1024, 1024)
        grad[side, pl.ds(r0, 512), :] = dg(normed2t[...], gh, 1, 0).astype(bf)
        grad[side, pl.ds(r0 + 512, 512), :] = dg(act, ct_v[...], 0, 0).astype(bf)
        vec[side, pl.ds(6 + j, 1), :] = jnp.sum(gh.astype(f32), 0, keepdims=True)
        return carry

    lax.fori_loop(0, 4, ffn, 0)
    red[1]["own"]()
    out_ref[...] = acc_o[...]

    vec[:, 12:16, :] = jnp.zeros((2, 4, 512), f32)
    vec[:, 8:12, :] = jnp.zeros((2, 4, 512), f32)
    for r in range(0, T, RB):
        gn = acc_g[r:r + RB, :]
        xh = xh2[r:r + RB, :]
        v = [jnp.sum(gn * xh, 0, keepdims=True), jnp.sum(gn, 0, keepdims=True)]
        h = gn * g2_ref[...]
        ct = ct_v[r:r + RB, :].astype(f32)
        g = ct + rs2[r // RB] * (h - jnp.mean(h, -1, keepdims=True) - xh * jnp.mean(h * xh, -1, keepdims=True))
        gm[r:r + RB, :] = g
        gb = g.astype(bf)
        normed2[r:r + RB, :] = gb
        v += [jnp.sum(gb.astype(f32), 0, keepdims=True), jnp.sum(ct, 0, keepdims=True)]
        for i, a in enumerate(v):
            a = a if r == 0 else vec[0, i:i + 1, :] + a
            vec[0, i:i + 1, :] = a
            vec[1, i:i + 1, :] = a
    red[1]["y"]()
    gb = normed2[...]
    for s in range(2):
        grad[s, 2048:2304, :] = dg(attb[s * 256:(s + 1) * 256, :], gb, 1, 0).astype(bf)
    red[2]["oth"]()
    red[2]["own"]()
    for s in range(2):
        acc_o[s * 256:(s + 1) * 256, :] = dg(ow[s], gb, 1, 1)

    row2 = lax.broadcasted_iota(jnp.int32, (AUG, T), 0)
    bwd_hooks = {
        1: [red[2]["y"]],
        4: [red[0]["x"]],
        6: [red[0]["z"]],
        7: [red[0]["agz"]],
    }

    def head_bwd(h, carry):
        run_hooks(bwd_hooks, h)
        hs = pl.ds(pl.multiple_of(h * 64, 64), 64)
        d = (acc_o[hs, :] * rr[pl.ds(h, 1), :]).astype(bf)
        dob[:64, :] = d
        dl = jnp.sum(d.astype(f32) * att[hs, :], 0, keepdims=True)
        hi = dl.astype(bf).astype(f32)
        dob[64:, :] = jnp.where(row2 == 0, -hi, jnp.where(row2 == 1, hi - dl, 0.0)).astype(bf)
        for q0 in range(0, T, QB):
            dp = dg(kv[h], dob[:, q0:q0 + QB], 0, 0)
            ds[:, q0:q0 + QB] = (dp * e_ref[h, :, q0:q0 + QB].astype(f32)).astype(bf)
        dq = dg(kk[h, :64, :], ds[...], 1, 0) * (1.0 / math.sqrt(HD))
        dk = dg(kq[h, :64, :], ds[...], 1, 1) * (1.0 / LOG2E)
        dv = dg(dob[:64, :], e_ref[h], 1, 1)
        b0 = pl.multiple_of(h * 192, 64)
        a, b = dq[:32], dq[32:]
        gp[pl.ds(b0, 32), :T] = (a * cos_v[0] + b * sin_v[0]).astype(bf)
        gp[pl.ds(b0 + 32, 32), :T] = (b * cos_v[0] - a * sin_v[0]).astype(bf)
        gp[pl.ds(b0, 64), T:] = jnp.zeros((64, A - T), bf)
        for i in range(2):
            sl = slice(i * T, (i + 1) * T)
            a, b = dk[:32, sl], dk[32:, sl]
            gp[pl.ds(b0 + 64, 32), sl] = (a * cos_v[i] + b * sin_v[i]).astype(bf)
            gp[pl.ds(b0 + 96, 32), sl] = (b * cos_v[i] - a * sin_v[i]).astype(bf)
        gp[pl.ds(b0 + 128, 64), :] = dv.astype(bf)
        return carry

    lax.fori_loop(0, H, head_bwd, 0)
    red[0]["agx"]()
    for s in (1, 0):
        grad[s, 2304:3072, :] = dg(gp[s * 768:(s + 1) * 768, :], normed[...], 1, 0).astype(bf)
        red[3]["oth" if s else "own"]()
    red[1]["x"]()
    red[3]["y"]()
    gn_oth[...] = (dg(gp[:768, T:], wt[0], 0, 0) + dg(gp[768:, T:], wt[1], 0, 0)).astype(bf)
    gn_cp().start()
    red[0]["agc"]()
    red[1]["z"]()
    qg = dg(jnp.ones((AUG, A), bf), gp[...], 1, 1)
    for h in range(H):
        vec[h // 4, 8 + h % 4:9 + h % 4, 0:192] = qg[0:1, h * 192:(h + 1) * 192]
    gn_own[...] = dg(gp[:768, :T], wt[0], 0, 0) + dg(gp[768:, :T], wt[1], 0, 0)
    for i, ref in enumerate((gn_own, gn_oth)):
        for r in range(0, T, RB):
            xh, _ = norm_rows(x_v[pl.ds(i * T + r, RB), :].astype(f32))
            gn = ref[r:r + RB, :].astype(f32)
            for j, a in enumerate((jnp.sum(gn * xh, 0, keepdims=True), jnp.sum(gn, 0, keepdims=True))):
                a = a if (r == 0 and i == 0) else vec[0, 4 + j:5 + j, :] + a
                vec[0, 4 + j:5 + j, :] = a
                vec[1, 4 + j:5 + j, :] = a
    v_core().start()
    red[1]["agz"]()
    red[2]["x"]()
    v_core().wait_recv()
    v_core().wait_send()
    vec[...] += vcr[...]
    v_y().start()
    red[2]["z"]()
    red[1]["agx"]()
    red[3]["x"]()
    red[2]["agz"]()
    red[1]["agc"]()
    red[3]["z"]()
    red[2]["agx"]()
    v_y().wait_recv()
    vec[0] = vec[0] + vyr[...]
    v_x().start()
    red[3]["agz"]()
    red[2]["agc"]()
    v_x().wait_recv()
    vzr[cm.z] = vec[0] + vxr[...]
    for c in v_z:
        c().start()
    red[3]["agx"]()
    gn_cp().wait_recv()
    for r in range(0, T, RB):
        xh, rs = norm_rows(x_v[r:r + RB, :].astype(f32))
        h = (gn_own[r:r + RB, :] + gn_in[r:r + RB, :].astype(f32)) * g1_ref[...]
        ig_ref[r:r + RB, :] = gm[r:r + RB, :] + rs * (h - jnp.mean(h, -1, keepdims=True) - xh * jnp.mean(h * xh, -1, keepdims=True))
    red[3]["agc"]()
    for c in v_z:
        c().wait_recv()
    vout_ref[...] = (vzr[0] + vzr[1]) + (vzr[2] + vzr[3])
    for k in range(4):
        red[k]["end"]()
    skip = cm.started.index(v_core)
    for i, make in enumerate(cm.started):
        if i != skip:
            make().wait_send()


N_SEM = 96


def call_mega(x, seg, g1, b1, wt, qb, ow, ob, g2, b2, iw, ib, dw, db, ct, cos, sin):
    A, D = x.shape
    T, R = A // 2, 768
    V = pl.BlockSpec(memory_space=pltpu.VMEM)
    N = pl.BlockSpec(memory_space=pl.ANY)
    S = jax.ShapeDtypeStruct
    outs = [S((T, D), f32), S((T, D), f32), S((ROWS_SIDE, D), bf), S((16, D), f32)]
    K = 64 + AUG
    shapes = [
        ((A, D), bf), ((T, D), bf), ((2, 32, T), f32), ((2, 32, T), f32), ((2, R, D), bf), ((2, 256, D), bf), ((2, D, 1024), bf), ((2, 1024, D), bf), ((16, 192), f32), ((16, 1024), f32),
        ((A, D), bf), ((D, A), bf), ((8, K, T), bf), ((8, K, A), bf), ((8, K, A), bf), ((8, A, T), bf), ((512, T), f32), ((512, T), bf), ((8, T), f32), ((K, T), bf), ((A, T), bf), ((2 * R, A), bf), ((T, D), bf), ((D, T), bf), ((T, D), f32), ((T, D), f32), ((T, D), f32), ((T, D), f32),
        ((2, ROWS_SIDE, D), bf), ((2, ROWS_SIDE // 2, D), bf), ((ROWS_SIDE // 2, D), bf), ((ROWS_SIDE // 4, D), bf), ((3, ROWS_SIDE // 16, D), bf), ((T, D), f32), ((T, D), bf), ((T, D), bf),
        ((2, 16, D), f32), ((2, 16, D), f32), ((16, D), f32), ((16, D), f32), ((4, 16, D), f32),
    ]
    scratch = [pltpu.VMEM(s, d) for s, d in shapes] + [pltpu.SemaphoreType.DMA((11,)), pltpu.SemaphoreType.DMA((N_SEM,)), pltpu.SemaphoreType.DMA((N_SEM,))]
    return pl.pallas_call(
        mega, out_shape=outs,
        in_specs=[N, V, V, V, N, V, N, V, V, V, N, V, N, V, N, N, N], out_specs=[V] * 4, scratch_shapes=scratch,
        compiler_params=pltpu.CompilerParams(vmem_limit_bytes=62 * 2**20, collective_id=0, has_side_effects=True),
    )(x, seg, g1, b1, wt, qb, ow, ob, g2, b2, iw, ib, dw, db, ct, cos, sin)


def finish(fin, vec, qkv, ow, iw, dw, qb, ib, *small):
    for j in range(2):
        iw[:, j * 512:(j + 1) * 512] = fin[j * 1024:j * 1024 + 512, :].astype(f32)
        dw[j * 512:(j + 1) * 512, :] = fin[j * 1024 + 512:(j + 1) * 1024, :].astype(f32)
        ib[:, j * 512:(j + 1) * 512] = vec[6 + j:7 + j, :]
    ow[...] = fin[2048:2304, :].astype(f32)
    qkv[...] = fin[2304:3072, :].astype(f32)
    qb[...] = vec[8:12, 0:192]
    for i, ref in enumerate(small):
        ref[...] = vec[i:i + 1, :]


def call_finish(fin, vec):
    D = fin.shape[1]
    V = pl.BlockSpec(memory_space=pltpu.VMEM)
    S = jax.ShapeDtypeStruct
    outs = [S(s, f32) for s in ((768, D), (256, D), (D, 1024), (1024, D), (4, 192), (1, 1024)) + ((1, D),) * 6]
    return pl.pallas_call(finish, out_shape=outs, in_specs=[V, V], out_specs=[V] * len(outs),
                          compiler_params=pltpu.CompilerParams(vmem_limit_bytes=40 * 2**20))(fin, vec)


def tables(length, half):
    fr = np.exp(np.arange(half, dtype=np.float64) * (-math.log(10000.0) / half))
    an = fr[:, None] * np.arange(length)[None, :]
    return np.cos(an).astype(np.float32), np.sin(an).astype(np.float32)


def local(inputs, seg, g1, b1, qkv_w, qkv_b, out_w, out_b, g2, b2, in_w, in_b, down_w, down_b, cot):
    A, D = inputs.shape[1:]
    cos, sin = tables(A, 32)
    r1 = lambda v: v.reshape(1, -1)
    wt = qkv_w.transpose(1, 2, 0).reshape(-1, D)
    out, ig, fin, vec = call_mega(inputs[0], seg, r1(g1), r1(b1), wt, qkv_b, out_w.reshape(-1, D), r1(out_b), r1(g2), r1(b2), in_w, r1(in_b), down_w, r1(down_b), cot[0], jnp.asarray(cos), jnp.asarray(sin))
    qkv, ow, iw, dw, qb, ib, *small = call_finish(fin, vec)
    ffn_gain, ffn_shift, out_bias, down_bias, attn_gain, attn_shift = (v.reshape(-1) for v in small)
    return (out[None], ig[None], attn_gain, attn_shift, qkv.reshape(4, 192, D).transpose(2, 0, 1), qb, ow.reshape(4, 64, D), out_bias, ffn_gain, ffn_shift, iw, ib.reshape(-1), dw, down_bias)


def normalize_rows(values):
    centered = values - jnp.mean(values, -1, keepdims=True)
    return centered * lax.rsqrt(jnp.mean(centered * centered, -1, keepdims=True) + EPS)


def gelu_exact(values):
    return jax.nn.gelu(values, approximate=False)


def rotate(vectors, count):
    half_size = vectors.shape[-1] // 2
    freq_index = jnp.arange(half_size, dtype=jnp.float32)
    frequency = jnp.exp(freq_index * (-math.log(10000.0) / half_size))
    angles = jnp.arange(count, dtype=jnp.float32)[:, None] * frequency[None, :]
    cosine = jnp.cos(angles)[:, None, :]
    sines = jnp.sin(angles)[:, None, :]
    lower_half = vectors[..., :half_size]
    upper_half = vectors[..., half_size:]
    return jnp.concatenate(
        [lower_half * cosine - upper_half * sines, upper_half * cosine + lower_half * sines], -1
    )


def arrange(projected):
    head_size = projected.shape[-1] // 3
    count = projected.shape[1]
    queries = rotate(projected[..., :head_size], count) * head_size ** (-0.5)
    rotated_keys = rotate(projected[..., head_size : 2 * head_size], count)
    return (queries, rotated_keys, projected[..., 2 * head_size :])


def block_scores(query_block, key_row, seg_block, seg_row):
    scores = jnp.einsum("qhe,khe->hqk", query_block, key_row, preferred_element_type=jnp.float32)
    same_gene = (seg_block[:, None] == seg_row[None, :])[None]
    return jnp.where(same_gene, scores, -1e30)


def attend_rows(queries, rotated_keys, values, segment_ids, block_rows):
    seq_length = queries.shape[1]
    block_count = seq_length // block_rows

    def one_row(row_args):
        query_row, key_row, value_row, seg_row = row_args

        def one_block(block_start):
            query_block = lax.dynamic_slice_in_dim(query_row, block_start, block_rows, 0)
            seg_block = lax.dynamic_slice_in_dim(seg_row, block_start, block_rows, 0)
            scores = block_scores(query_block, key_row, seg_block, seg_row)
            row_max = jnp.max(scores, -1, keepdims=True)
            exp_scores = jnp.exp(scores - row_max)
            row_total = jnp.sum(exp_scores, -1, keepdims=True)
            probability = (exp_scores / row_total).astype(jnp.bfloat16)
            block_out = jnp.einsum(
                "hqk,khe->qhe", probability, value_row, preferred_element_type=jnp.float32
            )
            return (block_out, (row_max + jnp.log(row_total))[..., 0])

        starts = jnp.arange(block_count, dtype=jnp.int32) * block_rows
        block_outs, log_totals = lax.map(one_block, starts)
        return (block_outs.reshape(seq_length, query_row.shape[1], query_row.shape[2]), log_totals)

    return lax.map(one_row, (queries, rotated_keys, values, segment_ids))


def attend_back(queries, rotated_keys, values, segment_ids, log_totals, grad_attended, block_rows):
    seq_length = queries.shape[1]
    block_count = seq_length // block_rows

    def one_row(row_args):
        query_row, key_row, value_row, seg_row, total_row, grad_row = row_args

        def one_block(carry, block_index):
            key_acc, value_acc = carry
            block_start = block_index * block_rows
            query_block = lax.dynamic_slice_in_dim(query_row, block_start, block_rows, 0)
            seg_block = lax.dynamic_slice_in_dim(seg_row, block_start, block_rows, 0)
            grad_block = lax.dynamic_slice_in_dim(grad_row, block_start, block_rows, 0)
            scores = block_scores(query_block, key_row, seg_block, seg_row)
            probability = jnp.exp(scores - total_row[block_index][..., None])
            grad_prob = jnp.einsum(
                "qhe,khe->hqk", grad_block, value_row, preferred_element_type=jnp.float32
            )
            delta = jnp.sum(probability * grad_prob, -1, keepdims=True)
            grad_scores = (probability * (grad_prob - delta)).astype(jnp.bfloat16)
            grad_query = jnp.einsum(
                "hqk,khe->qhe", grad_scores, key_row, preferred_element_type=jnp.float32
            )
            key_acc = key_acc + jnp.einsum(
                "hqk,qhe->khe", grad_scores, query_block, preferred_element_type=jnp.float32
            )
            value_acc = value_acc + jnp.einsum(
                "hqk,qhe->khe",
                probability.astype(jnp.bfloat16),
                grad_block,
                preferred_element_type=jnp.float32,
            )
            return ((key_acc, value_acc), grad_query)

        zeros_init = jnp.zeros(key_row.shape, jnp.float32)
        (grad_key, grad_value), grad_queries = lax.scan(
            one_block, (zeros_init, zeros_init), jnp.arange(block_count, dtype=jnp.int32)
        )
        return (grad_queries.reshape(key_row.shape), grad_key, grad_value)

    return lax.map(one_row, (queries, rotated_keys, values, segment_ids, log_totals, grad_attended))


def contract_rows(left, right):
    return lax.dot_general(
        left, right, (((0,), (0,)), ((), ())), preferred_element_type=jnp.float32
    )


def contract_cols(left, right):
    return lax.dot_general(
        left, right, (((1,), (1,)), ((), ())), preferred_element_type=jnp.float32
    )


def local_general(
    inputs,
    segment_ids,
    attention_norm_scale,
    attention_norm_bias,
    qkv_weight,
    qkv_bias,
    out_weight,
    out_bias,
    feedforward_norm_scale,
    feedforward_norm_bias,
    in_weight,
    in_bias,
    down_weight,
    down_bias,
    cotangent,
):
    row_count, seq_length, model_width = inputs.shape
    head_count = qkv_weight.shape[1]
    triple_size = qkv_weight.shape[2]
    head_size = triple_size // 3
    token_count = row_count * seq_length
    block_rows = min(512, seq_length)
    share_rows = seq_length // lax.axis_size("mp")
    share_start = lax.axis_index("mp") * share_rows

    def select_portion(array):
        return lax.dynamic_slice_in_dim(array, share_start, share_rows, 1)

    layer_input_rows = inputs.astype(jnp.float32)
    first_centered_scaled, first_deviation_backward = jax.vjp(normalize_rows, layer_input_rows)
    normed_reduced_precision = (
        first_centered_scaled * attention_norm_scale + attention_norm_bias
    ).astype(jnp.bfloat16)
    flat_normed = normed_reduced_precision.reshape(token_count, model_width)
    qkv_flat = qkv_weight.reshape(model_width, head_count * triple_size)
    projected = jnp.dot(flat_normed, qkv_flat, preferred_element_type=jnp.float32)
    projected = projected.reshape(row_count, seq_length, head_count, triple_size) + qkv_bias
    (queries, rotated_keys, values), arrange_pull = jax.vjp(arrange, projected)
    query_low = queries.astype(jnp.bfloat16)
    key_low = rotated_keys.astype(jnp.bfloat16)
    value_low = values.astype(jnp.bfloat16)
    attended, log_totals = attend_rows(query_low, key_low, value_low, segment_ids, block_rows)
    flat_attended = attended.astype(jnp.bfloat16).reshape(token_count, head_count * head_size)
    out_flat = out_weight.reshape(head_count * head_size, model_width)
    attn_part = jnp.dot(flat_attended, out_flat, preferred_element_type=jnp.float32)
    attn_part = attn_part.reshape(row_count, seq_length, model_width)
    attn_summed = lax.psum(attn_part, "mp")
    hidden_after_attention = layer_input_rows + attn_summed + out_bias
    second_centered_scaled, second_deviation_backward = jax.vjp(
        normalize_rows, hidden_after_attention
    )
    second_normed_rows = (
        second_centered_scaled * feedforward_norm_scale + feedforward_norm_bias
    ).astype(jnp.bfloat16)
    flat_two = second_normed_rows.reshape(token_count, model_width)
    hidden = jnp.dot(flat_two, in_weight, preferred_element_type=jnp.float32) + in_bias
    active, gelu_pull = jax.vjp(gelu_exact, hidden)
    active_low = active.astype(jnp.bfloat16)
    ffn_part = jnp.dot(active_low, down_weight, preferred_element_type=jnp.float32)
    ffn_part = ffn_part.reshape(row_count, seq_length, model_width)
    ffn_summed = lax.psum(ffn_part.astype(jnp.bfloat16), "mp").astype(jnp.float32)
    outputs = select_portion(hidden_after_attention + ffn_summed + down_bias)
    upstream = cotangent.astype(jnp.float32)
    flat_upstream = cotangent.reshape(token_count, model_width)
    down_bias_grad = jnp.sum(flat_upstream, 0, dtype=jnp.float32)
    down_weight_grad = contract_rows(active_low, flat_upstream)
    grad_active = contract_cols(flat_upstream, down_weight)
    grad_hidden = gelu_pull(grad_active)[0].astype(jnp.bfloat16)
    in_bias_grad = jnp.sum(grad_hidden, 0, dtype=jnp.float32)
    in_weight_grad = contract_rows(flat_two, grad_hidden)
    norm_two_part = contract_cols(grad_hidden, in_weight).reshape(
        row_count, seq_length, model_width
    )
    grad_normed_two = lax.psum(norm_two_part, "mp")
    grad_middle = upstream + second_deviation_backward(grad_normed_two * feedforward_norm_scale)[0]
    grad_branch = grad_middle.astype(jnp.bfloat16)
    second_norm_portion = select_portion(grad_normed_two)
    second_centered_portion = select_portion(second_centered_scaled)
    flat_branch = grad_branch.reshape(token_count, model_width)
    out_bias_grad = jnp.sum(flat_branch, 0, dtype=jnp.float32)
    out_weight_grad = contract_rows(flat_attended, flat_branch).reshape(
        head_count, head_size, model_width
    )
    grad_attended = contract_cols(flat_branch, out_flat).astype(jnp.bfloat16)
    grad_attended = grad_attended.reshape(row_count, seq_length, head_count, head_size)
    grad_query, grad_key, grad_value = attend_back(
        query_low, key_low, value_low, segment_ids, log_totals, grad_attended, block_rows
    )
    grad_projected = arrange_pull((grad_query, grad_key, grad_value))[0].astype(jnp.bfloat16)
    flat_projected = grad_projected.reshape(token_count, head_count * triple_size)
    qkv_bias_grad = jnp.sum(flat_projected, 0, dtype=jnp.float32).reshape(head_count, triple_size)
    qkv_weight_grad = contract_rows(flat_normed, flat_projected).reshape(
        model_width, head_count, triple_size
    )
    norm_one_part = contract_cols(flat_projected, qkv_flat).reshape(
        row_count, seq_length, model_width
    )
    grad_normed_one = lax.psum(norm_one_part.astype(jnp.bfloat16), "mp").astype(jnp.float32)
    input_grad = select_portion(
        grad_middle + first_deviation_backward(grad_normed_one * attention_norm_scale)[0]
    )
    first_norm_portion = select_portion(grad_normed_one)
    first_centered_portion = select_portion(first_centered_scaled)
    gain_terms = lax.psum(
        (
            jnp.sum(first_norm_portion * first_centered_portion, (0, 1)),
            jnp.sum(first_norm_portion, (0, 1)),
            jnp.sum(second_norm_portion * second_centered_portion, (0, 1)),
            jnp.sum(second_norm_portion, (0, 1)),
        ),
        ("dp", "mp"),
    )
    weight_terms = (
        lax.psum(qkv_weight_grad.astype(jnp.bfloat16), "dp").astype(jnp.float32),
        lax.psum(qkv_bias_grad.astype(jnp.bfloat16), "dp").astype(jnp.float32),
        lax.psum(out_weight_grad.astype(jnp.bfloat16), "dp").astype(jnp.float32),
        lax.psum(out_bias_grad.astype(jnp.bfloat16), "dp").astype(jnp.float32),
        lax.psum(in_weight_grad.astype(jnp.bfloat16), "dp").astype(jnp.float32),
        lax.psum(in_bias_grad.astype(jnp.bfloat16), "dp").astype(jnp.float32),
        lax.psum(down_weight_grad.astype(jnp.bfloat16), "dp").astype(jnp.float32),
        lax.psum(down_bias_grad.astype(jnp.bfloat16), "dp").astype(jnp.float32),
    )
    return (
        outputs,
        input_grad,
        gain_terms[0],
        gain_terms[1],
        weight_terms[0],
        weight_terms[1],
        weight_terms[2],
        weight_terms[3],
        gain_terms[2],
        gain_terms[3],
        weight_terms[4],
        weight_terms[5],
        weight_terms[6],
        weight_terms[7],
    )


def solution(mesh):
    return jax.shard_map(local if dict(mesh.shape) == {"dp": 16, "mp": 2} else local_general, mesh=mesh,
        in_specs=(P("dp", None, None), P("dp", None), P(), P(), P(None, "mp", None), P("mp", None), P("mp", None, None), P(), P(), P(), P(None, "mp"), P("mp"), P("mp", None), P(), P("dp", None, None)),
        out_specs=(P("dp", "mp", None), P("dp", "mp", None), P(), P(), P(None, "mp", None), P("mp", None), P("mp", None, None), P(), P(), P(), P(None, "mp"), P("mp"), P("mp", None), P()),
        check_vma=False)
```

```python
import functools
import math
import types

import jax
import jax.numpy as jnp
import numpy as np
from jax import lax
from jax.experimental import pallas as pl
from jax.experimental.pallas import tpu as pltpu
from jax.sharding import PartitionSpec as P

f32, bf = jnp.float32, jnp.bfloat16
EPS = 1e-5
BIG = 1e30
LOG2E = math.log2(math.e)
AUG = 16
ERFCX_P = 0.425
ERFCX = (
    0.23971980880709728, 0.24117083247455387, 0.20509840538640725, 0.239985627333635,
    -0.07373126048981057, 0.3746498195367672, -0.29358684214803077, 0.06669325662319364,
)
MESH = pl.DeviceIdType.MESH
CHUNKS = {
    "i0a": (0, 256, "xy"),
    "i0b": (256, 256, "xy"),
    "d0a": (512, 256, "yx"),
    "d0b": (768, 256, "xy"),
    "i1a": (1024, 256, "yx"),
    "i1b": (1280, 256, "xy"),
    "d1a": (1536, 256, "yx"),
    "d1b": (1792, 256, "xy"),
    "ow": (2048, 256, "yx"),
    "q0": (2304, 256, "xy"),
    "q1": (2560, 256, "yx"),
    "q2": (2816, 256, "yx"),
}
ROWS_SIDE = 3072
GATHER = {"wta": "s", "wtb": "s", "wo": "s", "wi0": "s", "wd0": "s", "wi1": "yxz", "wd1": "yzx"}
class Points:
    def F1_qkv(e):
        e.wta_x()

    def F1_mid(e):
        e.wta_z()

    def F2_start(e):
        e.wtb_x()
        e.wtb_z()
        e.wo_x()
        e.wo_z()
        e.wta_c()
        e.wi0_x()
        e.wta_r()
        e.qb_r()

    def F2_qkv(e):
        e.wtb_c()

    def F2_mid(e):
        e.wi0_z()
        e.wo_c()

    def F2_end(e):
        e.wd0_x()

    def F3_start(e):
        e.wtb_r()

    def F3_mid(e):
        e.wd0_z()

    def O_start(e):
        e.wo_r()

    def O_end(e):
        e.wi1_x()

    def M0_start(e):
        e.wi0_c()
        e.wd1_z()
        e.wi0_r()
        e.wd0_c()
        e.wi1_z()
        e.wd0_r()

    def M0_gelu(e):
        e.wd1_x()

    def M0_mid(e):
        e.d0b_oth()
        e.i0a_oth()
        e.i0b_oth()
        e.d0a_oth()

    def M1_gelu(e):
        e.d0b_xo()
        e.i0a_xo()
        e.d0a_y()
        e.i0b_xo()
        e.wi1_c()

    def M1_mid(e):
        e.d0b_own()
        e.i0a_own()
        e.i0b_own()
        e.d0a_own()

    def M2_start(e):
        e.wd1_c()
        e.wi1_r()
        e.d0b_xw()
        e.i0a_xw()
        e.i0b_xw()
        e.wd1_r()

    def M2_gelu(e):
        e.d0b_y()
        e.i0a_y()
        e.d0a_x()

    def M2_mid(e):
        e.i1a_oth()
        e.d1b_oth()
        e.i1b_oth()
        e.d1a_oth()

    def M2_end(e):
        e.i0b_y()

    def M3_gelu(e):
        e.i1a_y()
        e.d1b_xo()
        e.i1b_xo()
        e.d1a_y()
        e.d0b_z()

    def M3_mid(e):
        e.i1a_own()
        e.d1b_own()
        e.i1b_own()
        e.d1a_own()

    def M3_end(e):
        e.i0a_z()

    def W_end(e):
        e.d1b_xw()
        e.i0b_z()
        e.i1b_xw()
        e.ow_oth()
        e.ow_own()

    def B0_h1(e):
        e.d0a_z()
        e.d0b_az()

    def B0_h2(e):
        e.d1b_y()
        e.i1a_x()
        e.ow_y()
        e.i0a_az()

    def B0_h3(e):
        e.i1b_y()

    def B0_h4(e):
        e.i0b_az()

    def B0_end(e):
        e.q2_oth()
        e.q0_oth()
        e.q1_oth()
        e.d1a_x()
        e.d0a_az()

    def B1_h1(e):
        e.i1a_z()
        e.d1b_z()
        e.q2_y()
        e.d0b_ax()

    def B1_h2(e):
        e.q0_xo()
        e.q1_y()
        e.i0a_ax()

    def B1_h3(e):
        e.d1a_z()
        e.ow_x()
        e.i0b_ax()

    def B1_h4(e):
        e.i1b_z()
        e.d0b_ac()
        e.d0a_ax()

    def B1_end(e):
        e.q2_own()
        e.q0_own()
        e.q1_own()

    def G_oth(e):
        e.q0_y()
        e.d0b_end()
        e.gn_y()
        e.i1a_az()

    def G_own(e):
        e.q2_x()
        e.q0_xw()
        e.i0a_ac()
        e.d1b_az()

    def V_end(e):
        e.ow_z()
        e.v_c()
        e.d1a_az()

    def Z_end(e):
        e.i0a_end()
        e.q1_x()
        e.i0b_ac()
        e.i1b_az()
        e.v_y()
        e.i0b_end()
        e.d0a_ac()
        e.i1a_ax()
        e.d0a_end()
        e.q2_z()
        e.d1b_ax()
        e.q0_z()
        e.ow_az()
        e.q1_z()
        e.d1a_ax()
        e.i1a_ac()
        e.i1b_ax()
        e.i1a_end()
        e.d1b_ac()
        e.q2_az()
        e.d1b_end()
        e.d1a_ac()
        e.q0_az()
        e.d1a_end()
        e.i1b_ac()
        e.ow_ax()
        e.IG()
        e.i1b_end()
        e.v_x()
        e.q1_az()
        e.q2_ax()
        e.ow_ac()
        e.q0_ax()
        e.v_z()
        e.ow_end()
        e.q1_ax()
        e.q2_ac()
        e.q2_end()
        e.q0_ac()
        e.q0_end()
        e.v_end()
        e.q1_ac()
        e.q1_end()


FORDER = ((1, 0), (0, 0), (1, 1), (0, 1))


def dg(a, b, ca, cb):
    return lax.dot_general(a, b, (((ca,), (cb,)), ((), ())), preferred_element_type=f32)


def gelu_parts(u):
    ex = jnp.exp2(u * u * (-0.5 * LOG2E))
    t = 1.0 / (1.0 + (ERFCX_P / math.sqrt(2.0)) * jnp.abs(u))
    poly = 0.5 * ERFCX[-1]
    for c in ERFCX[-2::-1]:
        poly = poly * t + 0.5 * c
    tail = poly * t * ex
    phi_cum = jnp.where(u >= 0, 1.0 - tail, tail)
    return u * phi_cum, phi_cum + u * ex * (1.0 / math.sqrt(2 * math.pi))


def norm_rows(x):
    c = x - jnp.mean(x, -1, keepdims=True)
    rs = lax.rsqrt(jnp.mean(c * c, -1, keepdims=True) + EPS)
    return c * rs, rs


class Comm:
    def __init__(self, ssem, rsem):
        d, self.y = lax.axis_index("dp"), lax.axis_index("mp")
        self.z, self.x, self.c = d // 4, (d // 2) % 2, d % 2
        self.ssem, self.rsem, self.n_send, self.n_recv = ssem, rsem, 0, 0

    def dev(self, z=None, x=None, y=None, c=None):
        z, x, y, c = (b if a is None else a for a, b in ((z, self.z), (x, self.x), (y, self.y), (c, self.c)))
        return ((z * 2 + x) * 2 + c, y)

    def core(self):
        return self.dev(c=1 - self.c)

    def yy(self):
        return self.dev(y=1 - self.y)

    def xx(self):
        return self.dev(x=1 - self.x)

    def zz(self, k):
        return self.dev(z=lax.rem(self.z + k, 4))

    def partners(self):
        return [self.core(), self.yy(), self.xx()] + [self.zz(k) for k in (1, 2, 3)]

    def sems(self, n):
        self.n_send += n
        return list(range(self.n_send - n, self.n_send))

    def copy(self, src, dst, target, send, recv=None):
        if recv is None:
            recv = self.recv()

        def make():
            return pltpu.make_async_remote_copy(
                src_ref=src, dst_ref=dst, send_sem=self.ssem.at[send], recv_sem=self.rsem.at[recv],
                device_id=target, device_id_type=MESH)
        return make

    def recv(self):
        self.n_recv += 1
        return self.n_recv - 1


def rows(start, size):
    return pl.ds(pl.multiple_of(start, 16), size)


def mega(x_h, seg_ref, g1_ref, b1_ref, wt_h, qb_ref, ow_h, ob_ref, g2_ref, b2_ref, iw_h, ib_ref, dw_h, db_ref, ct_h, cos_h, sin_h,
         out_h, ig_h, fin_h, vout_ref,
         x_v, ct_v, cos_v, sin_v, wt, ow, iw, dw, qb, ib,
         normed, normed_t, kq, kk, kv, e_ref, att, attb, rr, dob, s0, s1, s0_bf, s1_bf, gp, normed2, normed2t, xh2, acc_o, acc_g, gm, act_v, gh_v, out_v, ig_v, fin_ref,
         grad, cr, yr, xr, zr, gn_own, gn_oth, gn_in, vec, vcr, vyr, vxr, vzr,
         lsem, ssem, rsem):
    A, D = x_v.shape
    T = ct_v.shape[0]
    HD = 64
    RB = 256
    cm = Comm(ssem, rsem)
    own0 = pl.multiple_of(cm.y * T, T)
    oth0 = pl.multiple_of((1 - cm.y) * T, T)

    barrier = pltpu.get_barrier_semaphore()
    for t in cm.partners():
        pl.semaphore_signal(barrier, inc=1, device_id=t, device_id_type=MESH)

    loads = [
        (x_h.at[pl.ds(own0, T)], x_v.at[pl.ds(0, T)]), (x_h.at[pl.ds(oth0, T)], x_v.at[pl.ds(T, T)]),
        (wt_h, wt.at[0]), (cos_h.at[:, pl.ds(own0, T)], cos_v.at[0]), (cos_h.at[:, pl.ds(oth0, T)], cos_v.at[1]),
        (sin_h.at[:, pl.ds(own0, T)], sin_v.at[0]), (sin_h.at[:, pl.ds(oth0, T)], sin_v.at[1]),
        (ow_h, ow.at[0]), (ct_h.at[pl.ds(own0, T)], ct_v), (iw_h, iw.at[0]), (dw_h, dw.at[0]),
    ]
    loads = [pltpu.make_async_copy(s, d, lsem.at[i]) for i, (s, d) in enumerate(loads)]
    for c in loads:
        c.start()
    stores = {}

    def store(name, src, dst):
        i = len(stores)
        stores[name] = lambda: pltpu.make_async_copy(src, dst, lsem.at[i])

    store("out", out_v, out_h)
    store("ig", ig_v, ig_h)
    for k, (r0, R, _) in CHUNKS.items():
        store(k, fin_ref.at[pl.ds(r0, R)], fin_h.at[pl.ds(r0, R)])
    qb[0:4, :] = qb_ref[...]
    ib[0:1, :] = ib_ref[...]

    ev = {}
    z0 = lax.rem(cm.z, 2)
    g_start, g_drain = [], []

    def zpair():
        return cm.dev(z=cm.z + 1 - 2 * z0)

    def piece(name, src, dst, cols, r0, total):
        kind = GATHER[name]
        e, h = total // 8, total // 2
        base = r0 + cm.c * h
        sa, sb = cm.sems(2)
        half = rows(base, h)

        def part(a, ref):
            return ref.at[a, cols]

        def cp(a, target, send, first=False):
            return cm.copy(part(a, src if first else dst), part(a, dst), target, send)

        if kind == "s":
            s = lax.rem(cm.x + z0, 2)
            pa, pb = rows(base + s * 2 * e, e), rows(base + s * 2 * e + e, e)
            ya, yb = cp(pa, cm.yy(), sa, True), cp(pb, cm.yy(), sb, True)
            xx, zz = cp(pa, cm.xx(), sa), cp(pb, zpair(), sb)
            cc = cp(half, cm.core(), sa)
            g_start.extend([ya, yb])

            def fx():
                ya().wait_recv()
                ya().wait_send()
                xx().start()

            def fz():
                yb().wait_recv()
                yb().wait_send()
                zz().start()

            def fc():
                xx().wait_recv()
                zz().wait_recv()
                xx().wait_send()
                cc().start()

            g_drain.extend([zz, cc])
        elif kind == "yx":
            pa = rows(base + cm.x * 2 * e, 2 * e)
            ya, xx = cp(pa, cm.yy(), sa, True), cp(pa, cm.xx(), sb)
            cc = cp(half, cm.core(), sa)
            g_start.append(ya)

            def fx():
                ya().wait_recv()
                xx().start()

            def fz():
                pass

            def fc():
                xx().wait_recv()
                ya().wait_send()
                cc().start()

            g_drain.extend([xx, cc])
        else:
            if kind == "yxz":
                pa, p2 = rows(base + z0 * 4 * e // 2 + cm.x * e, e), rows(base + z0 * 2 * e, 2 * e)
                t1, t2 = cm.xx(), zpair()
            else:
                pa, p2 = rows(base + cm.x * 2 * e + z0 * e, e), rows(base + cm.x * 2 * e, 2 * e)
                t1, t2 = zpair(), cm.xx()
            ya, one = cp(pa, cm.yy(), sa, True), cp(pa, t1, sb)
            two = cp(p2, t2, sa)
            cc = cp(half, cm.core(), sb)
            g_start.append(ya)

            def f1():
                ya().wait_recv()
                one().start()

            def f2():
                one().wait_recv()
                ya().wait_send()
                two().start()

            fx, fz = (f1, f2) if kind == "yxz" else (f2, f1)

            def fc():
                two().wait_recv()
                one().wait_send()
                cc().start()

            g_drain.extend([two, cc])
        ev.update({f"{name}_x": fx, f"{name}_z": fz, f"{name}_c": fc, f"{name}_r": lambda: cc().wait_recv()})

    full = pl.ds(0, D)
    piece("wta", wt_h, wt.at[1], full, 0, 384)
    g_qb = cm.copy(qb_ref, qb.at[pl.ds(8, 4)], cm.yy(), cm.sems(1)[0])
    g_ib = cm.copy(ib_ref, ib.at[pl.ds(8, 1)], cm.yy(), cm.sems(1)[0])
    g_start.extend([g_qb, g_ib])
    g_drain.extend([g_qb, g_ib])
    piece("wtb", wt_h, wt.at[1], full, 384, 384)
    piece("wo", ow_h, ow.at[1], full, 0, 256)
    for j in range(2):
        piece(f"wi{j}", iw_h, iw.at[1], pl.ds(j * 512, 512), 0, 512)
        piece(f"wd{j}", dw_h, dw.at[1], full, j * 512, 512)
    ev["qb_r"] = lambda: g_qb().wait_recv()

    def chunk_stages(k):
        r0, R, mode = CHUNKS[k]
        h, q, p = R // 2, R // 4, R // 16
        own, oth = grad.at[0], grad.at[1]
        lo = r0 + cm.c * h
        keep = rows(lo, h)
        give = rows(r0 + (1 - cm.c) * h, h)
        slot = rows(r0 // 2, h)
        qx, qo = lo + cm.x * q, lo + (1 - cm.x) * q
        qq, xslot, zslot = rows(qx, q), rows(r0 // 4, q), rows(r0 // 16, p)
        px = qx + cm.z * p
        sa, sb, sc = abc = cm.sems(3)
        core_oth = cm.copy(oth.at[give], cr.at[1, slot], cm.core(), sa)
        core_own = cm.copy(own.at[give], cr.at[0, slot], cm.core(), sb)
        rz, rg = cm.recv(), cm.recv()
        zs = [cm.copy(own.at[rows(qx + lax.rem(cm.z + j, 4) * p, p)], zr.at[j - 1, zslot], cm.zz(j), abc[j - 1], rz) for j in (1, 2, 3)]
        agz = [cm.copy(fin_ref.at[rows(px, p)], fin_ref.at[rows(px, p)], cm.zz(j), abc[j - 1], rg) for j in (1, 2, 3)]
        zs_all = cm.copy(zr.at[:, zslot], zr.at[:, zslot], cm.zz(1), sa, rz)
        agz_all = cm.copy(fin_ref.at[rows(r0, 3 * p)], fin_ref.at[rows(r0, 3 * p)], cm.zz(1), sa, rg)
        agx = cm.copy(fin_ref.at[qq], fin_ref.at[qq], cm.xx(), sa)
        agc = cm.copy(fin_ref.at[keep], fin_ref.at[keep], cm.core(), sb)

        def sent(*copies):
            for c in copies:
                c().wait_send()

        if mode == "yx":
            ycp = cm.copy(oth.at[keep], yr.at[slot], cm.yy(), sc)
            x_own = cm.copy(own.at[rows(qo, q)], xr.at[0, xslot], cm.xx(), sa)

            def s_y():
                core_oth().wait_recv()
                oth[keep] = (oth[keep].astype(f32) + cr[1, slot].astype(f32)).astype(bf)
                ycp().start()

            def s_x():
                core_own().wait_recv()
                ycp().wait_recv()
                own[keep] = (own[keep].astype(f32) + cr[0, slot].astype(f32) + yr[slot].astype(f32)).astype(bf)
                sent(core_oth)
                x_own().start()

            def s_z():
                x_own().wait_recv()
                own[qq] = (own[qq].astype(f32) + xr[0, xslot].astype(f32)).astype(bf)
                sent(x_own, core_own, ycp)
                for c in zs:
                    c().start()

            ev.update({f"{k}_y": s_y, f"{k}_x": s_x, f"{k}_z": s_z})
        else:
            yslot = rows(r0 // 2, q)
            x_oth = cm.copy(oth.at[rows(qo, q)], xr.at[1, xslot], cm.xx(), sa)
            x_own = cm.copy(own.at[rows(qo, q)], xr.at[0, xslot], cm.xx(), sb)
            ycp = cm.copy(oth.at[qq], yr.at[yslot], cm.yy(), sc)

            def s_xo():
                core_oth().wait_recv()
                oth[keep] = (oth[keep].astype(f32) + cr[1, slot].astype(f32)).astype(bf)
                sent(core_oth)
                x_oth().start()

            def s_xw():
                core_own().wait_recv()
                own[keep] = (own[keep].astype(f32) + cr[0, slot].astype(f32)).astype(bf)
                sent(core_own)
                x_own().start()

            def s_y():
                x_oth().wait_recv()
                oth[qq] = (oth[qq].astype(f32) + xr[1, xslot].astype(f32)).astype(bf)
                ycp().start()

            def s_z():
                x_own().wait_recv()
                ycp().wait_recv()
                own[qq] = (own[qq].astype(f32) + xr[0, xslot].astype(f32) + yr[yslot].astype(f32)).astype(bf)
                sent(x_oth, x_own, ycp)
                for c in zs:
                    c().start()

            ev.update({f"{k}_xo": s_xo, f"{k}_xw": s_xw, f"{k}_y": s_y, f"{k}_z": s_z})

        def s_az():
            zs_all().wait_recv()
            acc = own[rows(px, p)].astype(f32)
            for j in range(3):
                acc = acc + zr[j, zslot].astype(f32)
            fin_ref[rows(px, p)] = acc.astype(bf)
            sent(*zs)
            for c in agz:
                c().start()

        def s_ax():
            agz_all().wait_recv()
            sent(*agz)
            agx().start()

        def s_ac():
            agx().wait_recv()
            agc().start()

        def s_end():
            agc().wait_recv()
            sent(agx, agc)
            stores[k]().start()

        ev.update({f"{k}_oth": lambda: core_oth().start(), f"{k}_own": lambda: core_own().start(),
                   f"{k}_az": s_az, f"{k}_ax": s_ax, f"{k}_ac": s_ac, f"{k}_end": s_end})

    for k in CHUNKS:
        chunk_stages(k)
    gn_cp = cm.copy(gn_oth, gn_in, cm.yy(), cm.sems(1)[0])
    va, vb, vd = cm.sems(3)
    v_core = cm.copy(vec, vcr, cm.core(), va)
    v_y = cm.copy(vec.at[1], vyr, cm.yy(), va)
    v_x = cm.copy(vec.at[0], vxr, cm.xx(), va)
    rv = cm.recv()
    v_z = [cm.copy(vzr.at[cm.z], vzr.at[cm.z], cm.zz(j), (va, vb, vd)[j - 1], rv) for j in (1, 2, 3)]
    v_all = cm.copy(vzr.at[pl.ds(0, 3)], vzr.at[pl.ds(0, 3)], cm.zz(1), va, rv)

    def s_vy():
        v_core().wait_recv()
        v_core().wait_send()
        vec[...] += vcr[...]
        v_y().start()

    def s_vx():
        v_y().wait_recv()
        v_y().wait_send()
        vec[0] = vec[0] + vyr[...]
        v_x().start()

    def s_vz():
        v_x().wait_recv()
        v_x().wait_send()
        vzr[cm.z] = vec[0] + vxr[...]
        for c in v_z:
            c().start()

    def s_vend():
        v_all().wait_recv()
        vout_ref[...] = (vzr[0] + vzr[1]) + (vzr[2] + vzr[3])
        for c in v_z:
            c().wait_send()

    def s_ig():
        gn_cp().wait_recv()
        for r in range(0, T, RB):
            xh, rs = norm_rows(x_v[r:r + RB, :].astype(f32))
            h = (gn_own[r:r + RB, :] + gn_in[r:r + RB, :].astype(f32)) * g1_ref[...]
            ig_v[r:r + RB, :] = (gm[r:r + RB, :] + rs * (h - jnp.mean(h, -1, keepdims=True) - xh * jnp.mean(h * xh, -1, keepdims=True))).astype(bf)
        stores["ig"]().start()

    ev.update({"gn_y": lambda: gn_cp().start(), "v_c": lambda: v_core().start(), "v_y": s_vy, "v_x": s_vx, "v_z": s_vz, "v_end": s_vend, "IG": s_ig})
    assert cm.n_send <= N_SEND and cm.n_recv <= N_RECV, (cm.n_send, cm.n_recv)

    events = types.SimpleNamespace(**{k: f for k, f in ev.items()})

    def hook(name):
        point = getattr(Points, name, None)
        if point:
            point(events)

    def hook_at(names, index):
        for i, name in enumerate(names):
            if hasattr(Points, name):
                @pl.when(index == i)
                def _():
                    hook(name)

    def norm1(i):
        loads[i].wait()
        for r in range(0, T, RB):
            xh, _ = norm_rows(x_v[pl.ds(i * T + r, RB), :].astype(f32))
            normed[pl.ds(i * T + r, RB), :] = (xh * g1_ref[...] + b1_ref[...]).astype(bf)
        normed_t[:, i * T:(i + 1) * T] = normed[i * T:(i + 1) * T, :].T

    pl.semaphore_wait(barrier, 6)
    for mk in g_start:
        mk().start()
    norm1(0)
    norm1(1)

    row = lax.broadcasted_iota(jnp.int32, (AUG, T), 0)
    so = seg_ref[:, pl.ds(own0, T)]
    sth = seg_ref[:, pl.ds(oth0, T)]
    q_aug = jnp.where(row == so, 1.0, 0.0).astype(bf)
    k_aug = [jnp.where((row == s) | (row >= 4), 0.0, -BIG).astype(bf) for s in (so, sth)]
    v_aug = jnp.where(row < 2, 1.0, 0.0).astype(bf)
    for h in range(8):
        kq[h, 64:, :] = q_aug
        for i in range(2):
            kk[h, 64:, i * T:(i + 1) * T] = k_aug[i]
            kv[h, 64:, i * T:(i + 1) * T] = v_aug
    for i in range(2, 7):
        loads[i].wait()

    def pair_fwd(n, carry):
        names = [f"F{i}" for i in range(4)]
        hook_at([x + "_start" for x in names], n)
        side, hp = n // 2, lax.rem(n, 2)
        bias = qb[pl.ds(pl.multiple_of(side * 8, 8), 8), :]
        bias = jnp.where(hp == 0, bias[0:2], bias[2:4])
        w = wt[side, pl.ds(pl.multiple_of(hp * 384, 128), 384), :]
        bcol = [jnp.concatenate([jnp.broadcast_to(bias[i:i + 1, :], (128, 192)).T] * (T // 128), axis=1) for i in range(2)]
        for i in range(2):
            p2 = dg(w, normed_t[:, i * T:(i + 1) * T], 1, 0)
            cos, sin = cos_v[i], sin_v[i]
            sl = slice(i * T, (i + 1) * T)
            for hh in range(2):
                h = n * 2 + hh
                p = p2[hh * 192:(hh + 1) * 192] + bcol[hh]
                if i == 0:
                    a, b = p[0:32], p[32:64]
                    sc = LOG2E / math.sqrt(HD)
                    kq[h, 0:32, :] = ((a * cos - b * sin) * sc).astype(bf)
                    kq[h, 32:64, :] = ((b * cos + a * sin) * sc).astype(bf)
                a, b = p[64:96], p[96:128]
                kk[h, 0:32, sl] = (a * cos - b * sin).astype(bf)
                kk[h, 32:64, sl] = (b * cos + a * sin).astype(bf)
                kv[h, 0:64, sl] = p[128:].astype(bf)
        hook_at([x + "_qkv" for x in names], n)

        def scores(h, buf):
            buf[...] = dg(kk[h], kq[h], 0, 0)

        def soft(h, buf):
            s = buf[...]
            e = jnp.exp2(s - jnp.max(s, axis=0, keepdims=True)).astype(bf)
            e_ref[h] = e
            o = dg(kv[h], e, 1, 0)
            r = 1.0 / o[64:65]
            rr[pl.ds(h, 1), :] = r
            o = o[:64] * r
            hs = pl.ds(pl.multiple_of(h * 64, 64), 64)
            att[hs, :] = o
            attb[hs, :] = o.astype(bf)

        h = n * 2
        scores(h, s0)
        scores(h + 1, s1)
        soft(h, s0)
        hook_at([x + "_mid" for x in names], n)
        soft(h + 1, s1)
        hook_at([x + "_end" for x in names], n)
        return carry

    lax.fori_loop(0, 4, pair_fwd, 0)

    for i in (7, 8):
        loads[i].wait()
    hook("O_start")
    mid = x_v[0:T, :].astype(f32) + ob_ref[...]
    for s in range(2):
        mid = mid + dg(attb[s * 256:(s + 1) * 256, :], ow[s], 0, 0)
    acc_o[...] = mid
    rs2 = []
    for r in range(0, T, RB):
        xh, rs = norm_rows(acc_o[r:r + RB, :])
        rs2.append(rs)
        xh2[r:r + RB, :] = xh
        normed2[r:r + RB, :] = (xh * g2_ref[...] + b2_ref[...]).astype(bf)
    normed2t[...] = normed2[...].T
    acc_o[...] += db_ref[...]
    acc_g[...] = jnp.zeros_like(acc_g)
    for i in (9, 10):
        loads[i].wait()
    g_ib().wait_recv()
    hook("O_end")

    sides = [s for s, _ in FORDER]
    chunks = [j for _, j in FORDER]

    def pick(values, f):
        out = values[0]
        for i, v in enumerate(values[1:]):
            out = jnp.where(f == i + 1, v, out)
        return out

    def ffn(f, carry):
        hook_at([f"M{i}_start" for i in range(4)], f)
        side, j = pick(sides, f), pick(chunks, f)
        cols = pl.ds(pl.multiple_of(j * 512, 512), 512)
        r0 = pl.multiple_of(j * 1024, 1024)
        u = dg(normed2[...], iw[side, :, cols], 1, 0) + ib[pl.ds(side * 8, 1), cols]
        act, dge = gelu_parts(u)
        ga = dg(ct_v[...], dw[side, cols, :], 1, 1)
        act = act.astype(bf)
        act_v[...] = act
        gh = (ga * dge).astype(bf)
        gh_v[...] = gh
        vec[side, pl.ds(6 + j, 1), :] = jnp.sum(gh.astype(f32), 0, keepdims=True)
        hook_at([f"M{i}_gelu" for i in range(4)], f)
        grad[side, pl.ds(r0 + 512, 512), :] = dg(act_v[...], ct_v[...], 0, 0).astype(bf)
        grad[side, pl.ds(r0, 512), :] = dg(normed2t[...], gh_v[...], 1, 0).astype(bf)
        hook_at([f"M{i}_mid" for i in range(4)], f)
        acc_o[...] += dg(act_v[...], dw[side, cols, :], 1, 0)
        acc_g[...] += dg(gh_v[...], iw[side, :, cols], 1, 1)
        hook_at([f"M{i}_end" for i in range(4)], f)
        return carry

    lax.fori_loop(0, 4, ffn, 0)
    out_v[...] = acc_o[...].astype(bf)
    stores["out"]().start()

    vec[:, 8:16, :] = jnp.zeros((2, 8, 512), f32)
    for r in range(0, T, RB):
        gn = acc_g[r:r + RB, :]
        xh = xh2[r:r + RB, :]
        v = [jnp.sum(gn * xh, 0, keepdims=True), jnp.sum(gn, 0, keepdims=True)]
        h = gn * g2_ref[...]
        ct = ct_v[r:r + RB, :].astype(f32)
        g = ct + rs2[r // RB] * (h - jnp.mean(h, -1, keepdims=True) - xh * jnp.mean(h * xh, -1, keepdims=True))
        gm[r:r + RB, :] = g
        gb = g.astype(bf)
        normed2[r:r + RB, :] = gb
        v += [jnp.sum(gb.astype(f32), 0, keepdims=True), jnp.sum(ct, 0, keepdims=True)]
        for i, a in enumerate(v):
            a = a if r == 0 else vec[0, i:i + 1, :] + a
            vec[0, i:i + 1, :] = a
            vec[1, i:i + 1, :] = a
    hook("N_end")
    gb = normed2[...]
    for s in (1, 0):
        grad[s, 2048:2304, :] = dg(attb[s * 256:(s + 1) * 256, :], gb, 1, 0).astype(bf)
    for s in range(2):
        acc_o[s * 256:(s + 1) * 256, :] = dg(ow[s], gb, 1, 1)
    hook("W_end")

    row2 = lax.broadcasted_iota(jnp.int32, (AUG, T), 0)

    def side_bwd(n, carry):
        side = 1 - n
        hook_at(["B0_start", "B1_start"], n)

        def grad_scores(h, i, buf):
            hs = pl.ds(pl.multiple_of(h * 64, 64), 64)
            d = (acc_o[hs, :] * rr[pl.ds(h, 1), :]).astype(bf)
            dob[i, :64, :] = d
            dl = jnp.sum(d.astype(f32) * att[hs, :], 0, keepdims=True)
            hi = dl.astype(bf).astype(f32)
            dob[i, 64:, :] = jnp.where(row2 == 0, -hi, jnp.where(row2 == 1, hi - dl, 0.0)).astype(bf)
            dp = dg(kv[h], dob[i], 0, 0)
            buf[...] = (dp * e_ref[h].astype(f32)).astype(bf)

        def grads(h, i, buf):
            dq = dg(kk[h, :64, :], buf[...], 1, 0) * (1.0 / math.sqrt(HD))
            dk = dg(kq[h, :64, :], buf[...], 1, 1) * (1.0 / LOG2E)
            dv = dg(dob[i, :64, :], e_ref[h], 1, 1)
            b0 = pl.multiple_of(h * 192, 64)
            a, b = dq[:32], dq[32:]
            gp[pl.ds(b0, 32), :T] = (a * cos_v[0] + b * sin_v[0]).astype(bf)
            gp[pl.ds(b0 + 32, 32), :T] = (b * cos_v[0] - a * sin_v[0]).astype(bf)
            gp[pl.ds(b0, 64), T:] = jnp.zeros((64, A - T), bf)
            for k in range(2):
                sl = slice(k * T, (k + 1) * T)
                a, b = dk[:32, sl], dk[32:, sl]
                gp[pl.ds(b0 + 64, 32), sl] = (a * cos_v[k] + b * sin_v[k]).astype(bf)
                gp[pl.ds(b0 + 96, 32), sl] = (b * cos_v[k] - a * sin_v[k]).astype(bf)
            gp[pl.ds(b0 + 128, 64), :] = dv.astype(bf)

        d0, d1 = s0_bf, s1_bf
        h = side * 4
        grad_scores(h, 0, d0)
        grad_scores(h + 1, 1, d1)
        grads(h, 0, d0)
        hook_at(["B0_h1", "B1_h1"], n)
        grad_scores(h + 2, 0, d0)
        grads(h + 1, 1, d1)
        hook_at(["B0_h2", "B1_h2"], n)
        grad_scores(h + 3, 1, d1)
        grads(h + 2, 0, d0)
        hook_at(["B0_h3", "B1_h3"], n)
        grads(h + 3, 1, d1)
        hook_at(["B0_h4", "B1_h4"], n)
        g = gp[pl.ds(pl.multiple_of(side * 768, 256), 768), :]
        grad[side, 2304:3072, :] = dg(g, normed[...], 1, 0).astype(bf)
        hook_at(["B0_end", "B1_end"], n)
        return carry

    lax.fori_loop(0, 2, side_bwd, 0)
    gn_oth[...] = (dg(gp[:768, T:], wt[0], 0, 0) + dg(gp[768:, T:], wt[1], 0, 0)).astype(bf)
    hook("G_oth")
    gn_own[...] = dg(gp[:768, :T], wt[0], 0, 0) + dg(gp[768:, :T], wt[1], 0, 0)
    hook("G_own")
    qg = dg(jnp.ones((AUG, A), bf), gp[...], 1, 1)
    for h in range(8):
        vec[h // 4, 8 + h % 4:9 + h % 4, 0:192] = qg[0:1, h * 192:(h + 1) * 192]
    for i, ref in enumerate((gn_own, gn_oth)):
        for r in range(0, T, RB):
            xh, _ = norm_rows(x_v[pl.ds(i * T + r, RB), :].astype(f32))
            gn = ref[r:r + RB, :].astype(f32)
            for j, a in enumerate((jnp.sum(gn * xh, 0, keepdims=True), jnp.sum(gn, 0, keepdims=True))):
                a = a if (r == 0 and i == 0) else vec[0, 4 + j:5 + j, :] + a
                vec[0, 4 + j:5 + j, :] = a
                vec[1, 4 + j:5 + j, :] = a
    hook("V_end")
    hook("Z_end")
    for make in g_drain + [gn_cp]:
        make().wait_send()
    for st in stores.values():
        st().wait()


N_SEND, N_RECV = 20 + 3 * len(CHUNKS), 42 + 8 * len(CHUNKS) + sum(c[2] == "xy" for c in CHUNKS.values())


def call_mega(x, seg, g1, b1, wt, qb, ow, ob, g2, b2, iw, ib, dw, db, ct, cos, sin):
    A, D = x.shape
    T, R = A // 2, 768
    V = pl.BlockSpec(memory_space=pltpu.VMEM)
    N = pl.BlockSpec(memory_space=pl.ANY)
    S = jax.ShapeDtypeStruct
    outs = [S((T, D), bf), S((T, D), bf), S((ROWS_SIDE, D), bf), S((16, D), f32)]
    K = 64 + AUG
    shapes = [
        ((A, D), bf), ((T, D), bf), ((2, 32, T), f32), ((2, 32, T), f32), ((2, R, D), bf), ((2, 256, D), bf), ((2, D, 1024), bf), ((2, 1024, D), bf), ((16, 192), f32), ((16, 1024), f32),
        ((A, D), bf), ((D, A), bf), ((8, K, T), bf), ((8, K, A), bf), ((8, K, A), bf), ((8, A, T), bf), ((512, T), f32), ((512, T), bf), ((8, T), f32), ((2, K, T), bf), ((A, T), f32), ((A, T), f32), ((A, T), bf), ((A, T), bf), ((2 * R, A), bf), ((T, D), bf), ((D, T), bf), ((T, D), f32), ((T, D), f32), ((T, D), f32), ((T, D), f32), ((T, D), bf), ((T, D), bf), ((T, D), bf), ((T, D), bf), ((ROWS_SIDE, D), bf),
        ((2, ROWS_SIDE, D), bf), ((2, ROWS_SIDE // 2, D), bf), ((ROWS_SIDE // 2, D), bf), ((2, ROWS_SIDE // 4, D), bf), ((3, ROWS_SIDE // 16, D), bf), ((T, D), f32), ((T, D), bf), ((T, D), bf),
        ((2, 16, D), f32), ((2, 16, D), f32), ((16, D), f32), ((16, D), f32), ((4, 16, D), f32),
    ]
    scratch = [pltpu.VMEM(s, d) for s, d in shapes] + [pltpu.SemaphoreType.DMA((max(11, 2 + len(CHUNKS)),)), pltpu.SemaphoreType.DMA((N_SEND,)), pltpu.SemaphoreType.DMA((N_RECV,))]
    return pl.pallas_call(
        mega, out_shape=outs,
        in_specs=[N, V, V, V, N, V, N, V, V, V, N, V, N, V, N, N, N], out_specs=[N, N, N, V], scratch_shapes=scratch,
        compiler_params=pltpu.CompilerParams(vmem_limit_bytes=63 * 2**20, collective_id=0, has_side_effects=True),
    )(x, seg, g1, b1, wt, qb, ow, ob, g2, b2, iw, ib, dw, db, ct, cos, sin)


def finish(fin_h, out_h, ig_h, vec, out_f, ig_f, qkv_f, ow_f, iw_f, dw_f, qb, ib, g2, b2, ob, db, g1, b1, low, wide, isem, osem):
    D = out_h.shape[1]
    T = out_h.shape[0]
    parts = [(out_h, 0, T, out_f), (fin_h, 0, 512, iw_f.at[:, pl.ds(0, 512)]), (fin_h, 512, 512, dw_f.at[pl.ds(0, 512)]),
             (fin_h, 1024, 512, iw_f.at[:, pl.ds(512, 512)]), (fin_h, 1536, 512, dw_f.at[pl.ds(512, 512)]),
             (fin_h, 2048, 256, ow_f), (fin_h, 2304, 768, qkv_f), (ig_h, 0, T, ig_f)]
    at, ins, outs = 0, [], []
    for i, (src, r, n, dst) in enumerate(parts):
        here = pl.ds(at, n)
        ins.append((pltpu.make_async_copy(src.at[pl.ds(r, n)], low.at[here], isem.at[i]), here))
        outs.append(pltpu.make_async_copy(wide.at[here], dst, osem.at[i]))
        at += n
    for c, _ in ins:
        c.start()
    for j in range(2):
        ib[:, j * 512:(j + 1) * 512] = vec[6 + j:7 + j, :]
    qb[...] = vec[8:12, 0:192]
    for i, ref in enumerate((g2, b2, ob, db, g1, b1)):
        ref[...] = vec[i:i + 1, :]
    for (c, here), o in zip(ins, outs):
        c.wait()
        wide[here, :] = low[here, :].astype(f32)
        o.start()
    for o in outs:
        o.wait()


def call_finish(fin, out, ig, vec):
    T, D = out.shape
    V, N = pl.BlockSpec(memory_space=pltpu.VMEM), pl.BlockSpec(memory_space=pl.ANY)
    S = jax.ShapeDtypeStruct
    outs = [S(s, f32) for s in ((T, D), (T, D), (768, D), (256, D), (D, 1024), (1024, D), (4, 192), (1, 1024)) + ((1, D),) * 6]
    n = ROWS_SIDE + 2 * T
    return pl.pallas_call(finish, out_shape=outs, in_specs=[N, N, N, V], out_specs=[N] * 6 + [V] * 8,
                          scratch_shapes=[pltpu.VMEM((n, D), bf), pltpu.VMEM((n, D), f32), pltpu.SemaphoreType.DMA((8,)), pltpu.SemaphoreType.DMA((8,))],
                          compiler_params=pltpu.CompilerParams(vmem_limit_bytes=60 * 2**20))(fin, out, ig, vec)


def tables(length, half):
    fr = np.exp(np.arange(half, dtype=np.float64) * (-math.log(10000.0) / half))
    an = fr[:, None] * np.arange(length)[None, :]
    return np.cos(an).astype(np.float32), np.sin(an).astype(np.float32)


def local(inputs, seg, g1, b1, qkv_w, qkv_b, out_w, out_b, g2, b2, in_w, in_b, down_w, down_b, cot):
    A, D = inputs.shape[1:]
    cos, sin = tables(A, 32)
    r1 = lambda v: v.reshape(1, -1)
    wt = qkv_w.transpose(1, 2, 0).reshape(-1, D)
    out, ig, fin, vec = call_mega(inputs[0], seg, r1(g1), r1(b1), wt, qkv_b, out_w.reshape(-1, D), r1(out_b), r1(g2), r1(b2), in_w, r1(in_b), down_w, r1(down_b), cot[0], jnp.asarray(cos), jnp.asarray(sin))
    out, ig, qkv, ow, iw, dw, qb, ib, *small = call_finish(fin, out, ig, vec)
    ffn_gain, ffn_shift, out_bias, down_bias, attn_gain, attn_shift = (v.reshape(-1) for v in small)
    return (out[None], ig[None], attn_gain, attn_shift, qkv.reshape(4, 192, D).transpose(2, 0, 1), qb, ow.reshape(4, 64, D), out_bias, ffn_gain, ffn_shift, iw, ib.reshape(-1), dw, down_bias)


def normalize_rows(values):
    centered = values - jnp.mean(values, -1, keepdims=True)
    return centered * lax.rsqrt(jnp.mean(centered * centered, -1, keepdims=True) + EPS)


def gelu_exact(values):
    return jax.nn.gelu(values, approximate=False)


def rotate(vectors, count):
    half_size = vectors.shape[-1] // 2
    freq_index = jnp.arange(half_size, dtype=jnp.float32)
    frequency = jnp.exp(freq_index * (-math.log(10000.0) / half_size))
    angles = jnp.arange(count, dtype=jnp.float32)[:, None] * frequency[None, :]
    cosine = jnp.cos(angles)[:, None, :]
    sines = jnp.sin(angles)[:, None, :]
    lower_half = vectors[..., :half_size]
    upper_half = vectors[..., half_size:]
    return jnp.concatenate(
        [lower_half * cosine - upper_half * sines, upper_half * cosine + lower_half * sines], -1
    )


def arrange(projected):
    head_size = projected.shape[-1] // 3
    count = projected.shape[1]
    queries = rotate(projected[..., :head_size], count) * head_size ** (-0.5)
    rotated_keys = rotate(projected[..., head_size : 2 * head_size], count)
    return (queries, rotated_keys, projected[..., 2 * head_size :])


def block_scores(query_block, key_row, seg_block, seg_row):
    scores = jnp.einsum("qhe,khe->hqk", query_block, key_row, preferred_element_type=jnp.float32)
    same_gene = (seg_block[:, None] == seg_row[None, :])[None]
    return jnp.where(same_gene, scores, -1e30)


def attend_rows(queries, rotated_keys, values, segment_ids, block_rows):
    seq_length = queries.shape[1]
    block_count = seq_length // block_rows

    def one_row(row_args):
        query_row, key_row, value_row, seg_row = row_args

        def one_block(block_start):
            query_block = lax.dynamic_slice_in_dim(query_row, block_start, block_rows, 0)
            seg_block = lax.dynamic_slice_in_dim(seg_row, block_start, block_rows, 0)
            scores = block_scores(query_block, key_row, seg_block, seg_row)
            row_max = jnp.max(scores, -1, keepdims=True)
            exp_scores = jnp.exp(scores - row_max)
            row_total = jnp.sum(exp_scores, -1, keepdims=True)
            probability = (exp_scores / row_total).astype(jnp.bfloat16)
            block_out = jnp.einsum(
                "hqk,khe->qhe", probability, value_row, preferred_element_type=jnp.float32
            )
            return (block_out, (row_max + jnp.log(row_total))[..., 0])

        starts = jnp.arange(block_count, dtype=jnp.int32) * block_rows
        block_outs, log_totals = lax.map(one_block, starts)
        return (block_outs.reshape(seq_length, query_row.shape[1], query_row.shape[2]), log_totals)

    return lax.map(one_row, (queries, rotated_keys, values, segment_ids))


def attend_back(queries, rotated_keys, values, segment_ids, log_totals, grad_attended, block_rows):
    seq_length = queries.shape[1]
    block_count = seq_length // block_rows

    def one_row(row_args):
        query_row, key_row, value_row, seg_row, total_row, grad_row = row_args

        def one_block(carry, block_index):
            key_acc, value_acc = carry
            block_start = block_index * block_rows
            query_block = lax.dynamic_slice_in_dim(query_row, block_start, block_rows, 0)
            seg_block = lax.dynamic_slice_in_dim(seg_row, block_start, block_rows, 0)
            grad_block = lax.dynamic_slice_in_dim(grad_row, block_start, block_rows, 0)
            scores = block_scores(query_block, key_row, seg_block, seg_row)
            probability = jnp.exp(scores - total_row[block_index][..., None])
            grad_prob = jnp.einsum(
                "qhe,khe->hqk", grad_block, value_row, preferred_element_type=jnp.float32
            )
            delta = jnp.sum(probability * grad_prob, -1, keepdims=True)
            grad_scores = (probability * (grad_prob - delta)).astype(jnp.bfloat16)
            grad_query = jnp.einsum(
                "hqk,khe->qhe", grad_scores, key_row, preferred_element_type=jnp.float32
            )
            key_acc = key_acc + jnp.einsum(
                "hqk,qhe->khe", grad_scores, query_block, preferred_element_type=jnp.float32
            )
            value_acc = value_acc + jnp.einsum(
                "hqk,qhe->khe",
                probability.astype(jnp.bfloat16),
                grad_block,
                preferred_element_type=jnp.float32,
            )
            return ((key_acc, value_acc), grad_query)

        zeros_init = jnp.zeros(key_row.shape, jnp.float32)
        (grad_key, grad_value), grad_queries = lax.scan(
            one_block, (zeros_init, zeros_init), jnp.arange(block_count, dtype=jnp.int32)
        )
        return (grad_queries.reshape(key_row.shape), grad_key, grad_value)

    return lax.map(one_row, (queries, rotated_keys, values, segment_ids, log_totals, grad_attended))


def contract_rows(left, right):
    return lax.dot_general(
        left, right, (((0,), (0,)), ((), ())), preferred_element_type=jnp.float32
    )


def contract_cols(left, right):
    return lax.dot_general(
        left, right, (((1,), (1,)), ((), ())), preferred_element_type=jnp.float32
    )


def local_general(
    inputs,
    segment_ids,
    attention_norm_scale,
    attention_norm_bias,
    qkv_weight,
    qkv_bias,
    out_weight,
    out_bias,
    feedforward_norm_scale,
    feedforward_norm_bias,
    in_weight,
    in_bias,
    down_weight,
    down_bias,
    cotangent,
):
    row_count, seq_length, model_width = inputs.shape
    head_count = qkv_weight.shape[1]
    triple_size = qkv_weight.shape[2]
    head_size = triple_size // 3
    token_count = row_count * seq_length
    block_rows = min(512, seq_length)
    share_rows = seq_length // lax.axis_size("mp")
    share_start = lax.axis_index("mp") * share_rows

    def select_portion(array):
        return lax.dynamic_slice_in_dim(array, share_start, share_rows, 1)

    layer_input_rows = inputs.astype(jnp.float32)
    first_centered_scaled, first_deviation_backward = jax.vjp(normalize_rows, layer_input_rows)
    normed_reduced_precision = (
        first_centered_scaled * attention_norm_scale + attention_norm_bias
    ).astype(jnp.bfloat16)
    flat_normed = normed_reduced_precision.reshape(token_count, model_width)
    qkv_flat = qkv_weight.reshape(model_width, head_count * triple_size)
    projected = jnp.dot(flat_normed, qkv_flat, preferred_element_type=jnp.float32)
    projected = projected.reshape(row_count, seq_length, head_count, triple_size) + qkv_bias
    (queries, rotated_keys, values), arrange_pull = jax.vjp(arrange, projected)
    query_low = queries.astype(jnp.bfloat16)
    key_low = rotated_keys.astype(jnp.bfloat16)
    value_low = values.astype(jnp.bfloat16)
    attended, log_totals = attend_rows(query_low, key_low, value_low, segment_ids, block_rows)
    flat_attended = attended.astype(jnp.bfloat16).reshape(token_count, head_count * head_size)
    out_flat = out_weight.reshape(head_count * head_size, model_width)
    attn_part = jnp.dot(flat_attended, out_flat, preferred_element_type=jnp.float32)
    attn_part = attn_part.reshape(row_count, seq_length, model_width)
    attn_summed = lax.psum(attn_part, "mp")
    hidden_after_attention = layer_input_rows + attn_summed + out_bias
    second_centered_scaled, second_deviation_backward = jax.vjp(
        normalize_rows, hidden_after_attention
    )
    second_normed_rows = (
        second_centered_scaled * feedforward_norm_scale + feedforward_norm_bias
    ).astype(jnp.bfloat16)
    flat_two = second_normed_rows.reshape(token_count, model_width)
    hidden = jnp.dot(flat_two, in_weight, preferred_element_type=jnp.float32) + in_bias
    active, gelu_pull = jax.vjp(gelu_exact, hidden)
    active_low = active.astype(jnp.bfloat16)
    ffn_part = jnp.dot(active_low, down_weight, preferred_element_type=jnp.float32)
    ffn_part = ffn_part.reshape(row_count, seq_length, model_width)
    ffn_summed = lax.psum(ffn_part.astype(jnp.bfloat16), "mp").astype(jnp.float32)
    outputs = select_portion(hidden_after_attention + ffn_summed + down_bias)
    upstream = cotangent.astype(jnp.float32)
    flat_upstream = cotangent.reshape(token_count, model_width)
    down_bias_grad = jnp.sum(flat_upstream, 0, dtype=jnp.float32)
    down_weight_grad = contract_rows(active_low, flat_upstream)
    grad_active = contract_cols(flat_upstream, down_weight)
    grad_hidden = gelu_pull(grad_active)[0].astype(jnp.bfloat16)
    in_bias_grad = jnp.sum(grad_hidden, 0, dtype=jnp.float32)
    in_weight_grad = contract_rows(flat_two, grad_hidden)
    norm_two_part = contract_cols(grad_hidden, in_weight).reshape(
        row_count, seq_length, model_width
    )
    grad_normed_two = lax.psum(norm_two_part, "mp")
    grad_middle = upstream + second_deviation_backward(grad_normed_two * feedforward_norm_scale)[0]
    grad_branch = grad_middle.astype(jnp.bfloat16)
    second_norm_portion = select_portion(grad_normed_two)
    second_centered_portion = select_portion(second_centered_scaled)
    flat_branch = grad_branch.reshape(token_count, model_width)
    out_bias_grad = jnp.sum(flat_branch, 0, dtype=jnp.float32)
    out_weight_grad = contract_rows(flat_attended, flat_branch).reshape(
        head_count, head_size, model_width
    )
    grad_attended = contract_cols(flat_branch, out_flat).astype(jnp.bfloat16)
    grad_attended = grad_attended.reshape(row_count, seq_length, head_count, head_size)
    grad_query, grad_key, grad_value = attend_back(
        query_low, key_low, value_low, segment_ids, log_totals, grad_attended, block_rows
    )
    grad_projected = arrange_pull((grad_query, grad_key, grad_value))[0].astype(jnp.bfloat16)
    flat_projected = grad_projected.reshape(token_count, head_count * triple_size)
    qkv_bias_grad = jnp.sum(flat_projected, 0, dtype=jnp.float32).reshape(head_count, triple_size)
    qkv_weight_grad = contract_rows(flat_normed, flat_projected).reshape(
        model_width, head_count, triple_size
    )
    norm_one_part = contract_cols(flat_projected, qkv_flat).reshape(
        row_count, seq_length, model_width
    )
    grad_normed_one = lax.psum(norm_one_part.astype(jnp.bfloat16), "mp").astype(jnp.float32)
    input_grad = select_portion(
        grad_middle + first_deviation_backward(grad_normed_one * attention_norm_scale)[0]
    )
    first_norm_portion = select_portion(grad_normed_one)
    first_centered_portion = select_portion(first_centered_scaled)
    gain_terms = lax.psum(
        (
            jnp.sum(first_norm_portion * first_centered_portion, (0, 1)),
            jnp.sum(first_norm_portion, (0, 1)),
            jnp.sum(second_norm_portion * second_centered_portion, (0, 1)),
            jnp.sum(second_norm_portion, (0, 1)),
        ),
        ("dp", "mp"),
    )
    weight_terms = (
        lax.psum(qkv_weight_grad.astype(jnp.bfloat16), "dp").astype(jnp.float32),
        lax.psum(qkv_bias_grad.astype(jnp.bfloat16), "dp").astype(jnp.float32),
        lax.psum(out_weight_grad.astype(jnp.bfloat16), "dp").astype(jnp.float32),
        lax.psum(out_bias_grad.astype(jnp.bfloat16), "dp").astype(jnp.float32),
        lax.psum(in_weight_grad.astype(jnp.bfloat16), "dp").astype(jnp.float32),
        lax.psum(in_bias_grad.astype(jnp.bfloat16), "dp").astype(jnp.float32),
        lax.psum(down_weight_grad.astype(jnp.bfloat16), "dp").astype(jnp.float32),
        lax.psum(down_bias_grad.astype(jnp.bfloat16), "dp").astype(jnp.float32),
    )
    return (
        outputs,
        input_grad,
        gain_terms[0],
        gain_terms[1],
        weight_terms[0],
        weight_terms[1],
        weight_terms[2],
        weight_terms[3],
        gain_terms[2],
        gain_terms[3],
        weight_terms[4],
        weight_terms[5],
        weight_terms[6],
        weight_terms[7],
    )


def solution(mesh):
    return jax.shard_map(local if dict(mesh.shape) == {"dp": 16, "mp": 2} else local_general, mesh=mesh,
        in_specs=(P("dp", None, None), P("dp", None), P(), P(), P(None, "mp", None), P("mp", None), P("mp", None, None), P(), P(), P(), P(None, "mp"), P("mp"), P("mp", None), P(), P("dp", None, None)),
        out_specs=(P("dp", "mp", None), P("dp", "mp", None), P(), P(), P(None, "mp", None), P("mp", None), P("mp", None, None), P(), P(), P(), P(None, "mp"), P("mp"), P("mp", None), P()),
        check_vma=False)
```

```python
import functools
import math
import types

import jax
import jax.numpy as jnp
import numpy as np
from jax import lax
from jax.experimental import pallas as pl
from jax.experimental.pallas import tpu as pltpu
from jax.sharding import PartitionSpec as P

f32, bf = jnp.float32, jnp.bfloat16
EPS = 1e-5
BIG = 1e30
LOG2E = math.log2(math.e)
AUG = 16
ERFCX_P = 0.425
ERFCX = (
    0.23971980880709728, 0.24117083247455387, 0.20509840538640725, 0.239985627333635,
    -0.07373126048981057, 0.3746498195367672, -0.29358684214803077, 0.06669325662319364,
)
MESH = pl.DeviceIdType.MESH
CHUNKS = {
    "i0a": (0, 256, "xy"),
    "i0b": (256, 256, "xy"),
    "d0a": (512, 256, "yx"),
    "d0b": (768, 256, "xy"),
    "i1a": (1024, 256, "yx"),
    "i1b": (1280, 256, "xy"),
    "d1a": (1536, 256, "yx"),
    "d1b": (1792, 256, "xy"),
    "ow": (2048, 256, "yx"),
    "q0": (2304, 256, "xy"),
    "q1": (2560, 256, "yx"),
    "q2": (2816, 256, "yx"),
}
ROWS_SIDE = 3072
GATHER = {"wta": "s", "wtb": "s", "wo": "s", "wi0": "s", "wd0": "s", "wi1": "yxz", "wd1": "yzx"}
class Points:
    def F1_qkv(e):
        e.wta_x()

    def F1_mid(e):
        e.wta_z()

    def F2_start(e):
        e.wtb_x()
        e.wtb_z()
        e.wo_x()
        e.wo_z()
        e.wta_c()
        e.wi0_x()
        e.wta_r()
        e.qb_r()

    def F2_qkv(e):
        e.wtb_c()

    def F2_mid(e):
        e.wi0_z()
        e.wo_c()

    def F2_end(e):
        e.wd0_x()

    def F3_start(e):
        e.wtb_r()

    def F3_mid(e):
        e.wd0_z()

    def O_start(e):
        e.wo_r()

    def O_end(e):
        e.wi1_x()

    def M0_start(e):
        e.wi0_c()
        e.wd1_z()
        e.wi0_r()
        e.wd0_c()
        e.wi1_z()
        e.wd0_r()

    def M0_gelu(e):
        e.wd1_x()

    def M0_mid(e):
        e.d0b_oth()
        e.i0a_oth()
        e.i0b_oth()
        e.d0a_oth()

    def M1_gelu(e):
        e.d0b_xo()
        e.i0a_xo()
        e.d0a_y()
        e.i0b_xo()
        e.wi1_c()

    def M1_mid(e):
        e.d0b_own()
        e.i0a_own()
        e.i0b_own()
        e.d0a_own()

    def M2_start(e):
        e.wd1_c()
        e.wi1_r()
        e.d0b_xw()
        e.i0a_xw()
        e.i0b_xw()
        e.wd1_r()

    def M2_gelu(e):
        e.d0b_y()
        e.i0a_y()
        e.d0a_x()

    def M2_mid(e):
        e.i1a_oth()
        e.d1b_oth()
        e.i1b_oth()
        e.d1a_oth()

    def M2_end(e):
        e.i0b_y()

    def M3_gelu(e):
        e.i1a_y()
        e.d1b_xo()
        e.i1b_xo()
        e.d1a_y()
        e.d0b_z()

    def M3_mid(e):
        e.i1a_own()
        e.d1b_own()
        e.i1b_own()
        e.d1a_own()

    def M3_end(e):
        e.i0a_z()

    def W_end(e):
        e.d1b_xw()
        e.i0b_z()
        e.i1b_xw()
        e.ow_oth()
        e.ow_own()

    def B0_h1(e):
        e.d0a_z()
        e.d0b_az()

    def B0_h2(e):
        e.d1b_y()
        e.i1a_x()
        e.ow_y()
        e.i0a_az()

    def B0_h3(e):
        e.i1b_y()

    def B0_h4(e):
        e.i0b_az()

    def B0_end(e):
        e.q2_oth()
        e.q0_oth()
        e.q1_oth()
        e.d1a_x()
        e.d0a_az()

    def B1_h1(e):
        e.i1a_z()
        e.d1b_z()
        e.q2_y()
        e.d0b_ax()

    def B1_h2(e):
        e.q0_xo()
        e.q1_y()
        e.i0a_ax()

    def B1_h3(e):
        e.d1a_z()
        e.ow_x()
        e.i0b_ax()

    def B1_h4(e):
        e.i1b_z()
        e.d0b_ac()
        e.d0a_ax()

    def B1_end(e):
        e.q2_own()
        e.q0_own()
        e.q1_own()

    def G_oth(e):
        e.q0_y()
        e.d0b_end()
        e.gn_y()
        e.i1a_az()

    def G_own(e):
        e.q2_x()
        e.q0_xw()
        e.i0a_ac()
        e.d1b_az()

    def V_end(e):
        e.ow_z()
        e.v_c()
        e.d1a_az()

    def Z_end(e):
        e.i0a_end()
        e.q1_x()
        e.i0b_ac()
        e.i1b_az()
        e.v_y()
        e.i0b_end()
        e.d0a_ac()
        e.i1a_ax()
        e.d0a_end()
        e.q2_z()
        e.d1b_ax()
        e.q0_z()
        e.ow_az()
        e.q1_z()
        e.d1a_ax()
        e.i1a_ac()
        e.i1b_ax()
        e.i1a_end()
        e.d1b_ac()
        e.q2_az()
        e.d1b_end()
        e.d1a_ac()
        e.q0_az()
        e.d1a_end()
        e.i1b_ac()
        e.ow_ax()
        e.IG()
        e.i1b_end()
        e.v_x()
        e.q1_az()
        e.q2_ax()
        e.ow_ac()
        e.q0_ax()
        e.v_z()
        e.ow_end()
        e.q1_ax()
        e.q2_ac()
        e.q2_end()
        e.q0_ac()
        e.q0_end()
        e.v_end()
        e.q1_ac()
        e.q1_end()


FORDER = ((1, 0), (0, 0), (1, 1), (0, 1))


def dg(a, b, ca, cb):
    return lax.dot_general(a, b, (((ca,), (cb,)), ((), ())), preferred_element_type=f32)


def gelu_parts(u):
    ex = jnp.exp2(u * u * (-0.5 * LOG2E))
    t = 1.0 / (1.0 + (ERFCX_P / math.sqrt(2.0)) * jnp.abs(u))
    poly = 0.5 * ERFCX[-1]
    for c in ERFCX[-2::-1]:
        poly = poly * t + 0.5 * c
    tail = poly * t * ex
    phi_cum = jnp.where(u >= 0, 1.0 - tail, tail)
    return u * phi_cum, phi_cum + u * ex * (1.0 / math.sqrt(2 * math.pi))


def norm_rows(x):
    c = x - jnp.mean(x, -1, keepdims=True)
    rs = lax.rsqrt(jnp.mean(c * c, -1, keepdims=True) + EPS)
    return c * rs, rs


class Comm:
    def __init__(self, ssem, rsem):
        d, self.y = lax.axis_index("dp"), lax.axis_index("mp")
        self.z, self.x, self.c = d // 4, (d // 2) % 2, d % 2
        self.ssem, self.rsem, self.n_send, self.n_recv = ssem, rsem, 0, 0

    def dev(self, z=None, x=None, y=None, c=None):
        z, x, y, c = (b if a is None else a for a, b in ((z, self.z), (x, self.x), (y, self.y), (c, self.c)))
        return ((z * 2 + x) * 2 + c, y)

    def core(self):
        return self.dev(c=1 - self.c)

    def yy(self):
        return self.dev(y=1 - self.y)

    def xx(self):
        return self.dev(x=1 - self.x)

    def zz(self, k):
        return self.dev(z=lax.rem(self.z + k, 4))

    def partners(self):
        return [self.core(), self.yy(), self.xx()] + [self.zz(k) for k in (1, 2, 3)]

    def sems(self, n):
        self.n_send += n
        return list(range(self.n_send - n, self.n_send))

    def copy(self, src, dst, target, send, recv=None):
        if recv is None:
            recv = self.recv()

        def make():
            return pltpu.make_async_remote_copy(
                src_ref=src, dst_ref=dst, send_sem=self.ssem.at[send], recv_sem=self.rsem.at[recv],
                device_id=target, device_id_type=MESH)
        return make

    def recv(self):
        self.n_recv += 1
        return self.n_recv - 1


def rows(start, size):
    return pl.ds(pl.multiple_of(start, 16), size)


def mega(x_h, seg_ref, g1_ref, b1_ref, wt_h, qb_ref, ow_h, ob_ref, g2_ref, b2_ref, iw_h, ib_ref, dw_h, db_ref, ct_h, cos_h, sin_h,
         out_h, ig_h, fin_h, vout_ref,
         x_v, ct_v, cos_v, sin_v, wt, ow, iw, dw, qb, ib,
         normed, normed_t, kq, kk, kv, e_ref, att, attb, rr, dob, s0, s1, s0_bf, s1_bf, gp, normed2, normed2t, xh2, acc_o, acc_g, gm, act_v, gh_v, out_v, ig_v, fin_ref,
         grad, cr, yr, xr, zr, gn_own, gn_oth, gn_in, vec, vcr, vyr, vxr, vzr,
         lsem, ssem, rsem):
    A, D = x_v.shape
    T = ct_v.shape[0]
    HD = 64
    RB = 256
    cm = Comm(ssem, rsem)
    own0 = pl.multiple_of(cm.y * T, T)
    oth0 = pl.multiple_of((1 - cm.y) * T, T)

    barrier = pltpu.get_barrier_semaphore()
    for t in cm.partners():
        pl.semaphore_signal(barrier, inc=1, device_id=t, device_id_type=MESH)

    loads = [
        (x_h.at[pl.ds(own0, T)], x_v.at[pl.ds(0, T)]), (x_h.at[pl.ds(oth0, T)], x_v.at[pl.ds(T, T)]),
        (wt_h, wt.at[0]), (cos_h.at[:, pl.ds(own0, T)], cos_v.at[0]), (cos_h.at[:, pl.ds(oth0, T)], cos_v.at[1]),
        (sin_h.at[:, pl.ds(own0, T)], sin_v.at[0]), (sin_h.at[:, pl.ds(oth0, T)], sin_v.at[1]),
        (ow_h, ow.at[0]), (ct_h.at[pl.ds(own0, T)], ct_v), (iw_h, iw.at[0]), (dw_h, dw.at[0]),
    ]
    loads = [pltpu.make_async_copy(s, d, lsem.at[i]) for i, (s, d) in enumerate(loads)]
    for c in loads:
        c.start()
    stores = {}

    def store(name, src, dst):
        i = len(stores)
        stores[name] = lambda: pltpu.make_async_copy(src, dst, lsem.at[i])

    store("out", out_v, out_h)
    store("ig", ig_v, ig_h)
    for k, (r0, R, _) in CHUNKS.items():
        store(k, fin_ref.at[pl.ds(r0, R)], fin_h.at[pl.ds(r0, R)])
    qb[0:4, :] = qb_ref[...]
    ib[0:1, :] = ib_ref[...]

    ev = {}
    z0 = lax.rem(cm.z, 2)
    g_start, g_drain = [], []

    def zpair():
        return cm.dev(z=cm.z + 1 - 2 * z0)

    def piece(name, src, dst, cols, r0, total):
        kind = GATHER[name]
        e, h = total // 8, total // 2
        base = r0 + cm.c * h
        sa, sb = cm.sems(2)
        half = rows(base, h)

        def part(a, ref):
            return ref.at[a, cols]

        def cp(a, target, send, first=False):
            return cm.copy(part(a, src if first else dst), part(a, dst), target, send)

        if kind == "s":
            s = lax.rem(cm.x + z0, 2)
            pa, pb = rows(base + s * 2 * e, e), rows(base + s * 2 * e + e, e)
            ya, yb = cp(pa, cm.yy(), sa, True), cp(pb, cm.yy(), sb, True)
            xx, zz = cp(pa, cm.xx(), sa), cp(pb, zpair(), sb)
            cc = cp(half, cm.core(), sa)
            g_start.extend([ya, yb])

            def fx():
                ya().wait_recv()
                ya().wait_send()
                xx().start()

            def fz():
                yb().wait_recv()
                yb().wait_send()
                zz().start()

            def fc():
                xx().wait_recv()
                zz().wait_recv()
                xx().wait_send()
                cc().start()

            g_drain.extend([zz, cc])
        elif kind == "yx":
            pa = rows(base + cm.x * 2 * e, 2 * e)
            ya, xx = cp(pa, cm.yy(), sa, True), cp(pa, cm.xx(), sb)
            cc = cp(half, cm.core(), sa)
            g_start.append(ya)

            def fx():
                ya().wait_recv()
                xx().start()

            def fz():
                pass

            def fc():
                xx().wait_recv()
                ya().wait_send()
                cc().start()

            g_drain.extend([xx, cc])
        else:
            if kind == "yxz":
                pa, p2 = rows(base + z0 * 4 * e // 2 + cm.x * e, e), rows(base + z0 * 2 * e, 2 * e)
                t1, t2 = cm.xx(), zpair()
            else:
                pa, p2 = rows(base + cm.x * 2 * e + z0 * e, e), rows(base + cm.x * 2 * e, 2 * e)
                t1, t2 = zpair(), cm.xx()
            ya, one = cp(pa, cm.yy(), sa, True), cp(pa, t1, sb)
            two = cp(p2, t2, sa)
            cc = cp(half, cm.core(), sb)
            g_start.append(ya)

            def f1():
                ya().wait_recv()
                one().start()

            def f2():
                one().wait_recv()
                ya().wait_send()
                two().start()

            fx, fz = (f1, f2) if kind == "yxz" else (f2, f1)

            def fc():
                two().wait_recv()
                one().wait_send()
                cc().start()

            g_drain.extend([two, cc])
        ev.update({f"{name}_x": fx, f"{name}_z": fz, f"{name}_c": fc, f"{name}_r": lambda: cc().wait_recv()})

    full = pl.ds(0, D)
    piece("wta", wt_h, wt.at[1], full, 0, 384)
    g_qb = cm.copy(qb_ref, qb.at[pl.ds(8, 4)], cm.yy(), cm.sems(1)[0])
    g_ib = cm.copy(ib_ref, ib.at[pl.ds(8, 1)], cm.yy(), cm.sems(1)[0])
    g_start.extend([g_qb, g_ib])
    g_drain.extend([g_qb, g_ib])
    piece("wtb", wt_h, wt.at[1], full, 384, 384)
    piece("wo", ow_h, ow.at[1], full, 0, 256)
    for j in range(2):
        piece(f"wi{j}", iw_h, iw.at[1], pl.ds(j * 512, 512), 0, 512)
        piece(f"wd{j}", dw_h, dw.at[1], full, j * 512, 512)
    ev["qb_r"] = lambda: g_qb().wait_recv()

    def chunk_stages(k):
        r0, R, mode = CHUNKS[k]
        h, q, p = R // 2, R // 4, R // 16
        own, oth = grad.at[0], grad.at[1]
        lo = r0 + cm.c * h
        keep = rows(lo, h)
        give = rows(r0 + (1 - cm.c) * h, h)
        slot = rows(r0 // 2, h)
        qx, qo = lo + cm.x * q, lo + (1 - cm.x) * q
        qq, xslot, zslot = rows(qx, q), rows(r0 // 4, q), rows(r0 // 16, p)
        px = qx + cm.z * p
        sa, sb, sc = abc = cm.sems(3)
        core_oth = cm.copy(oth.at[give], cr.at[1, slot], cm.core(), sa)
        core_own = cm.copy(own.at[give], cr.at[0, slot], cm.core(), sb)
        rz, rg = cm.recv(), cm.recv()
        zs = [cm.copy(own.at[rows(qx + lax.rem(cm.z + j, 4) * p, p)], zr.at[j - 1, zslot], cm.zz(j), abc[j - 1], rz) for j in (1, 2, 3)]
        agz = [cm.copy(fin_ref.at[rows(px, p)], fin_ref.at[rows(px, p)], cm.zz(j), abc[j - 1], rg) for j in (1, 2, 3)]
        zs_all = cm.copy(zr.at[:, zslot], zr.at[:, zslot], cm.zz(1), sa, rz)
        agz_all = cm.copy(fin_ref.at[rows(r0, 3 * p)], fin_ref.at[rows(r0, 3 * p)], cm.zz(1), sa, rg)
        agx = cm.copy(fin_ref.at[qq], fin_ref.at[qq], cm.xx(), sa)
        agc = cm.copy(fin_ref.at[keep], fin_ref.at[keep], cm.core(), sb)

        def sent(*copies):
            for c in copies:
                c().wait_send()

        if mode == "yx":
            ycp = cm.copy(oth.at[keep], yr.at[slot], cm.yy(), sc)
            x_own = cm.copy(own.at[rows(qo, q)], xr.at[0, xslot], cm.xx(), sa)

            def s_y():
                core_oth().wait_recv()
                oth[keep] = (oth[keep].astype(f32) + cr[1, slot].astype(f32)).astype(bf)
                ycp().start()

            def s_x():
                core_own().wait_recv()
                ycp().wait_recv()
                own[keep] = (own[keep].astype(f32) + cr[0, slot].astype(f32) + yr[slot].astype(f32)).astype(bf)
                sent(core_oth)
                x_own().start()

            def s_z():
                x_own().wait_recv()
                own[qq] = (own[qq].astype(f32) + xr[0, xslot].astype(f32)).astype(bf)
                sent(x_own, core_own, ycp)
                for c in zs:
                    c().start()

            ev.update({f"{k}_y": s_y, f"{k}_x": s_x, f"{k}_z": s_z})
        else:
            yslot = rows(r0 // 2, q)
            x_oth = cm.copy(oth.at[rows(qo, q)], xr.at[1, xslot], cm.xx(), sa)
            x_own = cm.copy(own.at[rows(qo, q)], xr.at[0, xslot], cm.xx(), sb)
            ycp = cm.copy(oth.at[qq], yr.at[yslot], cm.yy(), sc)

            def s_xo():
                core_oth().wait_recv()
                oth[keep] = (oth[keep].astype(f32) + cr[1, slot].astype(f32)).astype(bf)
                sent(core_oth)
                x_oth().start()

            def s_xw():
                core_own().wait_recv()
                own[keep] = (own[keep].astype(f32) + cr[0, slot].astype(f32)).astype(bf)
                sent(core_own)
                x_own().start()

            def s_y():
                x_oth().wait_recv()
                oth[qq] = (oth[qq].astype(f32) + xr[1, xslot].astype(f32)).astype(bf)
                ycp().start()

            def s_z():
                x_own().wait_recv()
                ycp().wait_recv()
                own[qq] = (own[qq].astype(f32) + xr[0, xslot].astype(f32) + yr[yslot].astype(f32)).astype(bf)
                sent(x_oth, x_own, ycp)
                for c in zs:
                    c().start()

            ev.update({f"{k}_xo": s_xo, f"{k}_xw": s_xw, f"{k}_y": s_y, f"{k}_z": s_z})

        def s_az():
            zs_all().wait_recv()
            acc = own[rows(px, p)].astype(f32)
            for j in range(3):
                acc = acc + zr[j, zslot].astype(f32)
            fin_ref[rows(px, p)] = acc.astype(bf)
            sent(*zs)
            for c in agz:
                c().start()

        def s_ax():
            agz_all().wait_recv()
            sent(*agz)
            agx().start()

        def s_ac():
            agx().wait_recv()
            agc().start()

        def s_end():
            agc().wait_recv()
            sent(agx, agc)
            stores[k]().start()

        ev.update({f"{k}_oth": lambda: core_oth().start(), f"{k}_own": lambda: core_own().start(),
                   f"{k}_az": s_az, f"{k}_ax": s_ax, f"{k}_ac": s_ac, f"{k}_end": s_end})

    for k in CHUNKS:
        chunk_stages(k)
    gn_cp = cm.copy(gn_oth, gn_in, cm.yy(), cm.sems(1)[0])
    va, vb, vd = cm.sems(3)
    v_core = cm.copy(vec, vcr, cm.core(), va)
    v_y = cm.copy(vec.at[1], vyr, cm.yy(), va)
    v_x = cm.copy(vec.at[0], vxr, cm.xx(), va)
    rv = cm.recv()
    v_z = [cm.copy(vzr.at[cm.z], vzr.at[cm.z], cm.zz(j), (va, vb, vd)[j - 1], rv) for j in (1, 2, 3)]
    v_all = cm.copy(vzr.at[pl.ds(0, 3)], vzr.at[pl.ds(0, 3)], cm.zz(1), va, rv)

    def s_vy():
        v_core().wait_recv()
        v_core().wait_send()
        vec[...] += vcr[...]
        v_y().start()

    def s_vx():
        v_y().wait_recv()
        v_y().wait_send()
        vec[0] = vec[0] + vyr[...]
        v_x().start()

    def s_vz():
        v_x().wait_recv()
        v_x().wait_send()
        vzr[cm.z] = vec[0] + vxr[...]
        for c in v_z:
            c().start()

    def s_vend():
        v_all().wait_recv()
        vout_ref[...] = (vzr[0] + vzr[1]) + (vzr[2] + vzr[3])
        for c in v_z:
            c().wait_send()

    def s_ig():
        gn_cp().wait_recv()
        for r in range(0, T, RB):
            xh, rs = norm_rows(x_v[r:r + RB, :].astype(f32))
            h = (gn_own[r:r + RB, :] + gn_in[r:r + RB, :].astype(f32)) * g1_ref[...]
            ig_v[r:r + RB, :] = (gm[r:r + RB, :] + rs * (h - jnp.mean(h, -1, keepdims=True) - xh * jnp.mean(h * xh, -1, keepdims=True))).astype(bf)
        stores["ig"]().start()

    ev.update({"gn_y": lambda: gn_cp().start(), "v_c": lambda: v_core().start(), "v_y": s_vy, "v_x": s_vx, "v_z": s_vz, "v_end": s_vend, "IG": s_ig})
    assert cm.n_send <= N_SEND and cm.n_recv <= N_RECV, (cm.n_send, cm.n_recv)

    events = types.SimpleNamespace(**{k: f for k, f in ev.items()})

    def hook(name):
        point = getattr(Points, name, None)
        if point:
            point(events)

    def hook_at(names, index):
        for i, name in enumerate(names):
            if hasattr(Points, name):
                @pl.when(index == i)
                def _():
                    hook(name)

    def norm1(i):
        loads[i].wait()
        for r in range(0, T, RB):
            xh, _ = norm_rows(x_v[pl.ds(i * T + r, RB), :].astype(f32))
            normed[pl.ds(i * T + r, RB), :] = (xh * g1_ref[...] + b1_ref[...]).astype(bf)
        normed_t[:, i * T:(i + 1) * T] = normed[i * T:(i + 1) * T, :].T

    pl.semaphore_wait(barrier, 6)
    for mk in g_start:
        mk().start()
    norm1(0)
    norm1(1)

    row = lax.broadcasted_iota(jnp.int32, (AUG, T), 0)
    so = seg_ref[:, pl.ds(own0, T)]
    sth = seg_ref[:, pl.ds(oth0, T)]
    q_aug = jnp.where(row == so, 1.0, 0.0).astype(bf)
    k_aug = [jnp.where((row == s) | (row >= 4), 0.0, -BIG).astype(bf) for s in (so, sth)]
    v_aug = jnp.where(row < 2, 1.0, 0.0).astype(bf)
    for h in range(8):
        kq[h, 64:, :] = q_aug
        for i in range(2):
            kk[h, 64:, i * T:(i + 1) * T] = k_aug[i]
            kv[h, 64:, i * T:(i + 1) * T] = v_aug
    for i in range(2, 7):
        loads[i].wait()

    def pair_fwd(n, carry):
        names = [f"F{i}" for i in range(4)]
        hook_at([x + "_start" for x in names], n)
        side, hp = n // 2, lax.rem(n, 2)
        bias = qb[pl.ds(pl.multiple_of(side * 8, 8), 8), :]
        bias = jnp.where(hp == 0, bias[0:2], bias[2:4])
        w = wt[side, pl.ds(pl.multiple_of(hp * 384, 128), 384), :]
        bcol = [jnp.concatenate([jnp.broadcast_to(bias[i:i + 1, :], (128, 192)).T] * (T // 128), axis=1) for i in range(2)]
        for i in range(2):
            p2 = dg(w, normed_t[:, i * T:(i + 1) * T], 1, 0)
            cos, sin = cos_v[i], sin_v[i]
            sl = slice(i * T, (i + 1) * T)
            for hh in range(2):
                h = n * 2 + hh
                p = p2[hh * 192:(hh + 1) * 192] + bcol[hh]
                if i == 0:
                    a, b = p[0:32], p[32:64]
                    sc = LOG2E / math.sqrt(HD)
                    kq[h, 0:32, :] = ((a * cos - b * sin) * sc).astype(bf)
                    kq[h, 32:64, :] = ((b * cos + a * sin) * sc).astype(bf)
                a, b = p[64:96], p[96:128]
                kk[h, 0:32, sl] = (a * cos - b * sin).astype(bf)
                kk[h, 32:64, sl] = (b * cos + a * sin).astype(bf)
                kv[h, 0:64, sl] = p[128:].astype(bf)
        hook_at([x + "_qkv" for x in names], n)

        def scores(h, buf):
            buf[...] = dg(kk[h], kq[h], 0, 0)

        def soft(h, buf):
            s = buf[...]
            e = jnp.exp2(s - jnp.max(s, axis=0, keepdims=True)).astype(bf)
            e_ref[h] = e
            o = dg(kv[h], e, 1, 0)
            r = 1.0 / o[64:65]
            rr[pl.ds(h, 1), :] = r
            o = o[:64] * r
            hs = pl.ds(pl.multiple_of(h * 64, 64), 64)
            att[hs, :] = o
            attb[hs, :] = o.astype(bf)

        h = n * 2
        scores(h, s0)
        scores(h + 1, s1)
        soft(h, s0)
        hook_at([x + "_mid" for x in names], n)
        soft(h + 1, s1)
        hook_at([x + "_end" for x in names], n)
        return carry

    lax.fori_loop(0, 4, pair_fwd, 0)

    for i in (7, 8):
        loads[i].wait()
    hook("O_start")
    mid = x_v[0:T, :].astype(f32) + ob_ref[...]
    for s in range(2):
        mid = mid + dg(attb[s * 256:(s + 1) * 256, :], ow[s], 0, 0)
    acc_o[...] = mid
    rs2 = []
    for r in range(0, T, RB):
        xh, rs = norm_rows(acc_o[r:r + RB, :])
        rs2.append(rs)
        xh2[r:r + RB, :] = xh
        normed2[r:r + RB, :] = (xh * g2_ref[...] + b2_ref[...]).astype(bf)
    normed2t[...] = normed2[...].T
    acc_o[...] += db_ref[...]
    acc_g[...] = jnp.zeros_like(acc_g)
    for i in (9, 10):
        loads[i].wait()
    g_ib().wait_recv()
    hook("O_end")

    sides = [s for s, _ in FORDER]
    chunks = [j for _, j in FORDER]

    def pick(values, f):
        out = values[0]
        for i, v in enumerate(values[1:]):
            out = jnp.where(f == i + 1, v, out)
        return out

    def ffn(f, carry):
        hook_at([f"M{i}_start" for i in range(4)], f)
        side, j = pick(sides, f), pick(chunks, f)
        cols = pl.ds(pl.multiple_of(j * 512, 512), 512)
        r0 = pl.multiple_of(j * 1024, 1024)
        u = dg(normed2[...], iw[side, :, cols], 1, 0) + ib[pl.ds(side * 8, 1), cols]
        act, dge = gelu_parts(u)
        ga = dg(ct_v[...], dw[side, cols, :], 1, 1)
        act = act.astype(bf)
        act_v[...] = act
        gh = (ga * dge).astype(bf)
        gh_v[...] = gh
        vec[side, pl.ds(6 + j, 1), :] = jnp.sum(gh.astype(f32), 0, keepdims=True)
        hook_at([f"M{i}_gelu" for i in range(4)], f)
        grad[side, pl.ds(r0 + 512, 512), :] = dg(act_v[...], ct_v[...], 0, 0).astype(bf)
        grad[side, pl.ds(r0, 512), :] = dg(normed2t[...], gh_v[...], 1, 0).astype(bf)
        hook_at([f"M{i}_mid" for i in range(4)], f)
        acc_o[...] += dg(act_v[...], dw[side, cols, :], 1, 0)
        acc_g[...] += dg(gh_v[...], iw[side, :, cols], 1, 1)
        hook_at([f"M{i}_end" for i in range(4)], f)
        return carry

    lax.fori_loop(0, 4, ffn, 0)
    out_v[...] = acc_o[...].astype(bf)
    stores["out"]().start()

    vec[:, 8:16, :] = jnp.zeros((2, 8, 512), f32)
    for r in range(0, T, RB):
        gn = acc_g[r:r + RB, :]
        xh = xh2[r:r + RB, :]
        v = [jnp.sum(gn * xh, 0, keepdims=True), jnp.sum(gn, 0, keepdims=True)]
        h = gn * g2_ref[...]
        ct = ct_v[r:r + RB, :].astype(f32)
        g = ct + rs2[r // RB] * (h - jnp.mean(h, -1, keepdims=True) - xh * jnp.mean(h * xh, -1, keepdims=True))
        gm[r:r + RB, :] = g
        gb = g.astype(bf)
        normed2[r:r + RB, :] = gb
        v += [jnp.sum(gb.astype(f32), 0, keepdims=True), jnp.sum(ct, 0, keepdims=True)]
        for i, a in enumerate(v):
            a = a if r == 0 else vec[0, i:i + 1, :] + a
            vec[0, i:i + 1, :] = a
            vec[1, i:i + 1, :] = a
    hook("N_end")
    gb = normed2[...]
    for s in (1, 0):
        grad[s, 2048:2304, :] = dg(attb[s * 256:(s + 1) * 256, :], gb, 1, 0).astype(bf)
    for s in range(2):
        acc_o[s * 256:(s + 1) * 256, :] = dg(ow[s], gb, 1, 1)
    hook("W_end")

    row2 = lax.broadcasted_iota(jnp.int32, (AUG, T), 0)

    def side_bwd(n, carry):
        side = 1 - n
        hook_at(["B0_start", "B1_start"], n)

        def grad_scores(h, i, buf):
            hs = pl.ds(pl.multiple_of(h * 64, 64), 64)
            d = (acc_o[hs, :] * rr[pl.ds(h, 1), :]).astype(bf)
            dob[i, :64, :] = d
            dl = jnp.sum(d.astype(f32) * att[hs, :], 0, keepdims=True)
            hi = dl.astype(bf).astype(f32)
            dob[i, 64:, :] = jnp.where(row2 == 0, -hi, jnp.where(row2 == 1, hi - dl, 0.0)).astype(bf)
            dp = dg(kv[h], dob[i], 0, 0)
            buf[...] = (dp * e_ref[h].astype(f32)).astype(bf)

        def grads(h, i, buf):
            dq = dg(kk[h, :64, :], buf[...], 1, 0) * (1.0 / math.sqrt(HD))
            dk = dg(kq[h, :64, :], buf[...], 1, 1) * (1.0 / LOG2E)
            dv = dg(dob[i, :64, :], e_ref[h], 1, 1)
            b0 = pl.multiple_of(h * 192, 64)
            a, b = dq[:32], dq[32:]
            gp[pl.ds(b0, 32), :T] = (a * cos_v[0] + b * sin_v[0]).astype(bf)
            gp[pl.ds(b0 + 32, 32), :T] = (b * cos_v[0] - a * sin_v[0]).astype(bf)
            gp[pl.ds(b0, 64), T:] = jnp.zeros((64, A - T), bf)
            for k in range(2):
                sl = slice(k * T, (k + 1) * T)
                a, b = dk[:32, sl], dk[32:, sl]
                gp[pl.ds(b0 + 64, 32), sl] = (a * cos_v[k] + b * sin_v[k]).astype(bf)
                gp[pl.ds(b0 + 96, 32), sl] = (b * cos_v[k] - a * sin_v[k]).astype(bf)
            gp[pl.ds(b0 + 128, 64), :] = dv.astype(bf)

        d0, d1 = s0_bf, s1_bf
        h = side * 4
        grad_scores(h, 0, d0)
        grad_scores(h + 1, 1, d1)
        grads(h, 0, d0)
        hook_at(["B0_h1", "B1_h1"], n)
        grad_scores(h + 2, 0, d0)
        grads(h + 1, 1, d1)
        hook_at(["B0_h2", "B1_h2"], n)
        grad_scores(h + 3, 1, d1)
        grads(h + 2, 0, d0)
        hook_at(["B0_h3", "B1_h3"], n)
        grads(h + 3, 1, d1)
        hook_at(["B0_h4", "B1_h4"], n)
        g = gp[pl.ds(pl.multiple_of(side * 768, 256), 768), :]
        grad[side, 2304:3072, :] = dg(g, normed[...], 1, 0).astype(bf)
        hook_at(["B0_end", "B1_end"], n)
        return carry

    lax.fori_loop(0, 2, side_bwd, 0)
    gn_oth[...] = (dg(gp[:768, T:], wt[0], 0, 0) + dg(gp[768:, T:], wt[1], 0, 0)).astype(bf)
    hook("G_oth")
    gn_own[...] = dg(gp[:768, :T], wt[0], 0, 0) + dg(gp[768:, :T], wt[1], 0, 0)
    hook("G_own")
    qg = dg(jnp.ones((AUG, A), bf), gp[...], 1, 1)
    for h in range(8):
        vec[h // 4, 8 + h % 4:9 + h % 4, 0:192] = qg[0:1, h * 192:(h + 1) * 192]
    for i, ref in enumerate((gn_own, gn_oth)):
        for r in range(0, T, RB):
            xh, _ = norm_rows(x_v[pl.ds(i * T + r, RB), :].astype(f32))
            gn = ref[r:r + RB, :].astype(f32)
            for j, a in enumerate((jnp.sum(gn * xh, 0, keepdims=True), jnp.sum(gn, 0, keepdims=True))):
                a = a if (r == 0 and i == 0) else vec[0, 4 + j:5 + j, :] + a
                vec[0, 4 + j:5 + j, :] = a
                vec[1, 4 + j:5 + j, :] = a
    hook("V_end")
    hook("Z_end")
    for make in g_drain + [gn_cp]:
        make().wait_send()
    for st in stores.values():
        st().wait()


N_SEND, N_RECV = 20 + 3 * len(CHUNKS), 42 + 8 * len(CHUNKS) + sum(c[2] == "xy" for c in CHUNKS.values())


def call_mega(x, seg, g1, b1, wt, qb, ow, ob, g2, b2, iw, ib, dw, db, ct, cos, sin):
    A, D = x.shape
    T, R = A // 2, 768
    V = pl.BlockSpec(memory_space=pltpu.VMEM)
    N = pl.BlockSpec(memory_space=pl.ANY)
    S = jax.ShapeDtypeStruct
    outs = [S((T, D), bf), S((T, D), bf), S((ROWS_SIDE, D), bf), S((16, D), f32)]
    K = 64 + AUG
    shapes = [
        ((A, D), bf), ((T, D), bf), ((2, 32, T), f32), ((2, 32, T), f32), ((2, R, D), bf), ((2, 256, D), bf), ((2, D, 1024), bf), ((2, 1024, D), bf), ((16, 192), f32), ((16, 1024), f32),
        ((A, D), bf), ((D, A), bf), ((8, K, T), bf), ((8, K, A), bf), ((8, K, A), bf), ((8, A, T), bf), ((512, T), f32), ((512, T), bf), ((8, T), f32), ((2, K, T), bf), ((A, T), f32), ((A, T), f32), ((A, T), bf), ((A, T), bf), ((2 * R, A), bf), ((T, D), bf), ((D, T), bf), ((T, D), f32), ((T, D), f32), ((T, D), f32), ((T, D), f32), ((T, D), bf), ((T, D), bf), ((T, D), bf), ((T, D), bf), ((ROWS_SIDE, D), bf),
        ((2, ROWS_SIDE, D), bf), ((2, ROWS_SIDE // 2, D), bf), ((ROWS_SIDE // 2, D), bf), ((2, ROWS_SIDE // 4, D), bf), ((3, ROWS_SIDE // 16, D), bf), ((T, D), f32), ((T, D), bf), ((T, D), bf),
        ((2, 16, D), f32), ((2, 16, D), f32), ((16, D), f32), ((16, D), f32), ((4, 16, D), f32),
    ]
    scratch = [pltpu.VMEM(s, d) for s, d in shapes] + [pltpu.SemaphoreType.DMA((max(11, 2 + len(CHUNKS)),)), pltpu.SemaphoreType.DMA((N_SEND,)), pltpu.SemaphoreType.DMA((N_RECV,))]
    return pl.pallas_call(
        mega, out_shape=outs,
        in_specs=[N, V, V, V, N, V, N, V, V, V, N, V, N, V, N, N, N], out_specs=[N, N, N, V], scratch_shapes=scratch,
        compiler_params=pltpu.CompilerParams(vmem_limit_bytes=63 * 2**20, collective_id=0, has_side_effects=True),
    )(x, seg, g1, b1, wt, qb, ow, ob, g2, b2, iw, ib, dw, db, ct, cos, sin)


def finish(fin_h, out_h, ig_h, vec, out_f, ig_f, qkv_f, ow_f, iw_f, dw_f, qb, ib, g2, b2, ob, db, g1, b1, low, wide, isem, osem):
    D = out_h.shape[1]
    T = out_h.shape[0]
    parts = [(out_h, 0, T, out_f), (fin_h, 0, 512, iw_f.at[:, pl.ds(0, 512)]), (fin_h, 512, 512, dw_f.at[pl.ds(0, 512)]),
             (fin_h, 1024, 512, iw_f.at[:, pl.ds(512, 512)]), (fin_h, 1536, 512, dw_f.at[pl.ds(512, 512)]),
             (fin_h, 2048, 256, ow_f), (fin_h, 2304, 768, qkv_f), (ig_h, 0, T, ig_f)]
    at, ins, outs = 0, [], []
    for i, (src, r, n, dst) in enumerate(parts):
        here = pl.ds(at, n)
        ins.append((pltpu.make_async_copy(src.at[pl.ds(r, n)], low.at[here], isem.at[i]), here))
        outs.append(pltpu.make_async_copy(wide.at[here], dst, osem.at[i]))
        at += n
    for c, _ in ins:
        c.start()
    for j in range(2):
        ib[:, j * 512:(j + 1) * 512] = vec[6 + j:7 + j, :]
    qb[...] = vec[8:12, 0:192]
    for i, ref in enumerate((g2, b2, ob, db, g1, b1)):
        ref[...] = vec[i:i + 1, :]
    for i, ((c, here), o) in enumerate(zip(ins, outs)):
        c.wait()
        wide[here, :] = low[here, :].astype(f32)
        o.start(priority=i % 2)
    for o in outs:
        o.wait()


def call_finish(fin, out, ig, vec):
    T, D = out.shape
    V, N = pl.BlockSpec(memory_space=pltpu.VMEM), pl.BlockSpec(memory_space=pl.ANY)
    S = jax.ShapeDtypeStruct
    outs = [S(s, f32) for s in ((T, D), (T, D), (768, D), (256, D), (D, 1024), (1024, D), (4, 192), (1, 1024)) + ((1, D),) * 6]
    n = ROWS_SIDE + 2 * T
    return pl.pallas_call(finish, out_shape=outs, in_specs=[N, N, N, V], out_specs=[N] * 6 + [V] * 8,
                          scratch_shapes=[pltpu.VMEM((n, D), bf), pltpu.VMEM((n, D), f32), pltpu.SemaphoreType.DMA((8,)), pltpu.SemaphoreType.DMA((8,))],
                          compiler_params=pltpu.CompilerParams(vmem_limit_bytes=60 * 2**20))(fin, out, ig, vec)


def tables(length, half):
    fr = np.exp(np.arange(half, dtype=np.float64) * (-math.log(10000.0) / half))
    an = fr[:, None] * np.arange(length)[None, :]
    return np.cos(an).astype(np.float32), np.sin(an).astype(np.float32)


def local(inputs, seg, g1, b1, qkv_w, qkv_b, out_w, out_b, g2, b2, in_w, in_b, down_w, down_b, cot):
    A, D = inputs.shape[1:]
    cos, sin = tables(A, 32)
    r1 = lambda v: v.reshape(1, -1)
    wt = qkv_w.transpose(1, 2, 0).reshape(-1, D)
    out, ig, fin, vec = call_mega(inputs[0], seg, r1(g1), r1(b1), wt, qkv_b, out_w.reshape(-1, D), r1(out_b), r1(g2), r1(b2), in_w, r1(in_b), down_w, r1(down_b), cot[0], jnp.asarray(cos), jnp.asarray(sin))
    out, ig, qkv, ow, iw, dw, qb, ib, *small = call_finish(fin, out, ig, vec)
    ffn_gain, ffn_shift, out_bias, down_bias, attn_gain, attn_shift = (v.reshape(-1) for v in small)
    return (out[None], ig[None], attn_gain, attn_shift, qkv.reshape(4, 192, D).transpose(2, 0, 1), qb, ow.reshape(4, 64, D), out_bias, ffn_gain, ffn_shift, iw, ib.reshape(-1), dw, down_bias)


def normalize_rows(values):
    centered = values - jnp.mean(values, -1, keepdims=True)
    return centered * lax.rsqrt(jnp.mean(centered * centered, -1, keepdims=True) + EPS)


def gelu_exact(values):
    return jax.nn.gelu(values, approximate=False)


def rotate(vectors, count):
    half_size = vectors.shape[-1] // 2
    freq_index = jnp.arange(half_size, dtype=jnp.float32)
    frequency = jnp.exp(freq_index * (-math.log(10000.0) / half_size))
    angles = jnp.arange(count, dtype=jnp.float32)[:, None] * frequency[None, :]
    cosine = jnp.cos(angles)[:, None, :]
    sines = jnp.sin(angles)[:, None, :]
    lower_half = vectors[..., :half_size]
    upper_half = vectors[..., half_size:]
    return jnp.concatenate(
        [lower_half * cosine - upper_half * sines, upper_half * cosine + lower_half * sines], -1
    )


def arrange(projected):
    head_size = projected.shape[-1] // 3
    count = projected.shape[1]
    queries = rotate(projected[..., :head_size], count) * head_size ** (-0.5)
    rotated_keys = rotate(projected[..., head_size : 2 * head_size], count)
    return (queries, rotated_keys, projected[..., 2 * head_size :])


def block_scores(query_block, key_row, seg_block, seg_row):
    scores = jnp.einsum("qhe,khe->hqk", query_block, key_row, preferred_element_type=jnp.float32)
    same_gene = (seg_block[:, None] == seg_row[None, :])[None]
    return jnp.where(same_gene, scores, -1e30)


def attend_rows(queries, rotated_keys, values, segment_ids, block_rows):
    seq_length = queries.shape[1]
    block_count = seq_length // block_rows

    def one_row(row_args):
        query_row, key_row, value_row, seg_row = row_args

        def one_block(block_start):
            query_block = lax.dynamic_slice_in_dim(query_row, block_start, block_rows, 0)
            seg_block = lax.dynamic_slice_in_dim(seg_row, block_start, block_rows, 0)
            scores = block_scores(query_block, key_row, seg_block, seg_row)
            row_max = jnp.max(scores, -1, keepdims=True)
            exp_scores = jnp.exp(scores - row_max)
            row_total = jnp.sum(exp_scores, -1, keepdims=True)
            probability = (exp_scores / row_total).astype(jnp.bfloat16)
            block_out = jnp.einsum(
                "hqk,khe->qhe", probability, value_row, preferred_element_type=jnp.float32
            )
            return (block_out, (row_max + jnp.log(row_total))[..., 0])

        starts = jnp.arange(block_count, dtype=jnp.int32) * block_rows
        block_outs, log_totals = lax.map(one_block, starts)
        return (block_outs.reshape(seq_length, query_row.shape[1], query_row.shape[2]), log_totals)

    return lax.map(one_row, (queries, rotated_keys, values, segment_ids))


def attend_back(queries, rotated_keys, values, segment_ids, log_totals, grad_attended, block_rows):
    seq_length = queries.shape[1]
    block_count = seq_length // block_rows

    def one_row(row_args):
        query_row, key_row, value_row, seg_row, total_row, grad_row = row_args

        def one_block(carry, block_index):
            key_acc, value_acc = carry
            block_start = block_index * block_rows
            query_block = lax.dynamic_slice_in_dim(query_row, block_start, block_rows, 0)
            seg_block = lax.dynamic_slice_in_dim(seg_row, block_start, block_rows, 0)
            grad_block = lax.dynamic_slice_in_dim(grad_row, block_start, block_rows, 0)
            scores = block_scores(query_block, key_row, seg_block, seg_row)
            probability = jnp.exp(scores - total_row[block_index][..., None])
            grad_prob = jnp.einsum(
                "qhe,khe->hqk", grad_block, value_row, preferred_element_type=jnp.float32
            )
            delta = jnp.sum(probability * grad_prob, -1, keepdims=True)
            grad_scores = (probability * (grad_prob - delta)).astype(jnp.bfloat16)
            grad_query = jnp.einsum(
                "hqk,khe->qhe", grad_scores, key_row, preferred_element_type=jnp.float32
            )
            key_acc = key_acc + jnp.einsum(
                "hqk,qhe->khe", grad_scores, query_block, preferred_element_type=jnp.float32
            )
            value_acc = value_acc + jnp.einsum(
                "hqk,qhe->khe",
                probability.astype(jnp.bfloat16),
                grad_block,
                preferred_element_type=jnp.float32,
            )
            return ((key_acc, value_acc), grad_query)

        zeros_init = jnp.zeros(key_row.shape, jnp.float32)
        (grad_key, grad_value), grad_queries = lax.scan(
            one_block, (zeros_init, zeros_init), jnp.arange(block_count, dtype=jnp.int32)
        )
        return (grad_queries.reshape(key_row.shape), grad_key, grad_value)

    return lax.map(one_row, (queries, rotated_keys, values, segment_ids, log_totals, grad_attended))


def contract_rows(left, right):
    return lax.dot_general(
        left, right, (((0,), (0,)), ((), ())), preferred_element_type=jnp.float32
    )


def contract_cols(left, right):
    return lax.dot_general(
        left, right, (((1,), (1,)), ((), ())), preferred_element_type=jnp.float32
    )


def local_general(
    inputs,
    segment_ids,
    attention_norm_scale,
    attention_norm_bias,
    qkv_weight,
    qkv_bias,
    out_weight,
    out_bias,
    feedforward_norm_scale,
    feedforward_norm_bias,
    in_weight,
    in_bias,
    down_weight,
    down_bias,
    cotangent,
):
    row_count, seq_length, model_width = inputs.shape
    head_count = qkv_weight.shape[1]
    triple_size = qkv_weight.shape[2]
    head_size = triple_size // 3
    token_count = row_count * seq_length
    block_rows = min(512, seq_length)
    share_rows = seq_length // lax.axis_size("mp")
    share_start = lax.axis_index("mp") * share_rows

    def select_portion(array):
        return lax.dynamic_slice_in_dim(array, share_start, share_rows, 1)

    layer_input_rows = inputs.astype(jnp.float32)
    first_centered_scaled, first_deviation_backward = jax.vjp(normalize_rows, layer_input_rows)
    normed_reduced_precision = (
        first_centered_scaled * attention_norm_scale + attention_norm_bias
    ).astype(jnp.bfloat16)
    flat_normed = normed_reduced_precision.reshape(token_count, model_width)
    qkv_flat = qkv_weight.reshape(model_width, head_count * triple_size)
    projected = jnp.dot(flat_normed, qkv_flat, preferred_element_type=jnp.float32)
    projected = projected.reshape(row_count, seq_length, head_count, triple_size) + qkv_bias
    (queries, rotated_keys, values), arrange_pull = jax.vjp(arrange, projected)
    query_low = queries.astype(jnp.bfloat16)
    key_low = rotated_keys.astype(jnp.bfloat16)
    value_low = values.astype(jnp.bfloat16)
    attended, log_totals = attend_rows(query_low, key_low, value_low, segment_ids, block_rows)
    flat_attended = attended.astype(jnp.bfloat16).reshape(token_count, head_count * head_size)
    out_flat = out_weight.reshape(head_count * head_size, model_width)
    attn_part = jnp.dot(flat_attended, out_flat, preferred_element_type=jnp.float32)
    attn_part = attn_part.reshape(row_count, seq_length, model_width)
    attn_summed = lax.psum(attn_part, "mp")
    hidden_after_attention = layer_input_rows + attn_summed + out_bias
    second_centered_scaled, second_deviation_backward = jax.vjp(
        normalize_rows, hidden_after_attention
    )
    second_normed_rows = (
        second_centered_scaled * feedforward_norm_scale + feedforward_norm_bias
    ).astype(jnp.bfloat16)
    flat_two = second_normed_rows.reshape(token_count, model_width)
    hidden = jnp.dot(flat_two, in_weight, preferred_element_type=jnp.float32) + in_bias
    active, gelu_pull = jax.vjp(gelu_exact, hidden)
    active_low = active.astype(jnp.bfloat16)
    ffn_part = jnp.dot(active_low, down_weight, preferred_element_type=jnp.float32)
    ffn_part = ffn_part.reshape(row_count, seq_length, model_width)
    ffn_summed = lax.psum(ffn_part.astype(jnp.bfloat16), "mp").astype(jnp.float32)
    outputs = select_portion(hidden_after_attention + ffn_summed + down_bias)
    upstream = cotangent.astype(jnp.float32)
    flat_upstream = cotangent.reshape(token_count, model_width)
    down_bias_grad = jnp.sum(flat_upstream, 0, dtype=jnp.float32)
    down_weight_grad = contract_rows(active_low, flat_upstream)
    grad_active = contract_cols(flat_upstream, down_weight)
    grad_hidden = gelu_pull(grad_active)[0].astype(jnp.bfloat16)
    in_bias_grad = jnp.sum(grad_hidden, 0, dtype=jnp.float32)
    in_weight_grad = contract_rows(flat_two, grad_hidden)
    norm_two_part = contract_cols(grad_hidden, in_weight).reshape(
        row_count, seq_length, model_width
    )
    grad_normed_two = lax.psum(norm_two_part, "mp")
    grad_middle = upstream + second_deviation_backward(grad_normed_two * feedforward_norm_scale)[0]
    grad_branch = grad_middle.astype(jnp.bfloat16)
    second_norm_portion = select_portion(grad_normed_two)
    second_centered_portion = select_portion(second_centered_scaled)
    flat_branch = grad_branch.reshape(token_count, model_width)
    out_bias_grad = jnp.sum(flat_branch, 0, dtype=jnp.float32)
    out_weight_grad = contract_rows(flat_attended, flat_branch).reshape(
        head_count, head_size, model_width
    )
    grad_attended = contract_cols(flat_branch, out_flat).astype(jnp.bfloat16)
    grad_attended = grad_attended.reshape(row_count, seq_length, head_count, head_size)
    grad_query, grad_key, grad_value = attend_back(
        query_low, key_low, value_low, segment_ids, log_totals, grad_attended, block_rows
    )
    grad_projected = arrange_pull((grad_query, grad_key, grad_value))[0].astype(jnp.bfloat16)
    flat_projected = grad_projected.reshape(token_count, head_count * triple_size)
    qkv_bias_grad = jnp.sum(flat_projected, 0, dtype=jnp.float32).reshape(head_count, triple_size)
    qkv_weight_grad = contract_rows(flat_normed, flat_projected).reshape(
        model_width, head_count, triple_size
    )
    norm_one_part = contract_cols(flat_projected, qkv_flat).reshape(
        row_count, seq_length, model_width
    )
    grad_normed_one = lax.psum(norm_one_part.astype(jnp.bfloat16), "mp").astype(jnp.float32)
    input_grad = select_portion(
        grad_middle + first_deviation_backward(grad_normed_one * attention_norm_scale)[0]
    )
    first_norm_portion = select_portion(grad_normed_one)
    first_centered_portion = select_portion(first_centered_scaled)
    gain_terms = lax.psum(
        (
            jnp.sum(first_norm_portion * first_centered_portion, (0, 1)),
            jnp.sum(first_norm_portion, (0, 1)),
            jnp.sum(second_norm_portion * second_centered_portion, (0, 1)),
            jnp.sum(second_norm_portion, (0, 1)),
        ),
        ("dp", "mp"),
    )
    weight_terms = (
        lax.psum(qkv_weight_grad.astype(jnp.bfloat16), "dp").astype(jnp.float32),
        lax.psum(qkv_bias_grad.astype(jnp.bfloat16), "dp").astype(jnp.float32),
        lax.psum(out_weight_grad.astype(jnp.bfloat16), "dp").astype(jnp.float32),
        lax.psum(out_bias_grad.astype(jnp.bfloat16), "dp").astype(jnp.float32),
        lax.psum(in_weight_grad.astype(jnp.bfloat16), "dp").astype(jnp.float32),
        lax.psum(in_bias_grad.astype(jnp.bfloat16), "dp").astype(jnp.float32),
        lax.psum(down_weight_grad.astype(jnp.bfloat16), "dp").astype(jnp.float32),
        lax.psum(down_bias_grad.astype(jnp.bfloat16), "dp").astype(jnp.float32),
    )
    return (
        outputs,
        input_grad,
        gain_terms[0],
        gain_terms[1],
        weight_terms[0],
        weight_terms[1],
        weight_terms[2],
        weight_terms[3],
        gain_terms[2],
        gain_terms[3],
        weight_terms[4],
        weight_terms[5],
        weight_terms[6],
        weight_terms[7],
    )


def solution(mesh):
    return jax.shard_map(local if dict(mesh.shape) == {"dp": 16, "mp": 2} else local_general, mesh=mesh,
        in_specs=(P("dp", None, None), P("dp", None), P(), P(), P(None, "mp", None), P("mp", None), P("mp", None, None), P(), P(), P(), P(None, "mp"), P("mp"), P("mp", None), P(), P("dp", None, None)),
        out_specs=(P("dp", "mp", None), P("dp", "mp", None), P(), P(), P(None, "mp", None), P("mp", None), P("mp", None, None), P(), P(), P(), P(None, "mp"), P("mp"), P("mp", None), P()),
        check_vma=False)
```
